32 devices in a mesh: paths: 2 (over x), node: 16 (over z, y, core).
Axes of the slice: x: 2, y: 2, z: 4, core: 2. Of those that a mesh axis runs over, the one named last changes fastest.
Arguments:
- amplitudes: float32 [2, 2097152], P(None, ('paths', 'node')), parts along dimension 1, may hold values from -6 to 6
- gates: float32 [2, 12, 128, 128], replicated, may hold values from -0.375 to 0.375
Outputs:
- final_state: float32 [2, 2097152], P(None, ('paths', 'node')), parts along dimension 1
The draws below stay inside these ranges and needn't reach their ends.
There are 2 independent parts, one for each index of `paths`. The reference program is written for one: setup_inputs(seed, part) draws one part's arguments, and reference() takes and returns one part's arrays. A program takes and returns all parts, laid end to end along the dimension named above; an argument that names none is the same for every part. Nothing has to cross between parts.
All inputs are finite; a program needn't handle non-finite values.
Results may differ from the reference program's by a relative error of at most 0.0001.
Values sent between devices are 32-bit elements; how exact they have to be, the bound alone decides.
No kernel may reach another device: no remote copies, remote signals or barrier semaphores. Data moves between devices by JAX's collectives and lax.ppermute only.
A program may use at most 64 MiB of HBM per device.

```python
import jax
import jax.numpy as jnp
from jax import lax

LOC = 65536
GORDER = 128
GATES = 12
AMPS = 1048576
N_NODE = 16


def shard_levels(stream_key, extent, pieces, smallest, largest):
    gain, own = 1.0, jax.random.fold_in(stream_key, 6)
    for axis_at, shards_of in pieces:
        heights = jnp.exp(jax.random.uniform(jax.random.fold_in(own, axis_at), (shards_of,), jnp.float32, smallest / len(pieces), largest / len(pieces)))
        gain = gain * jnp.repeat(heights, extent[axis_at] // shards_of).reshape([-1 if axis == axis_at else 1 for axis in range(len(extent))])
    return gain


def normal_values(key, dims, scale, reach, pieces=(), dtype=jnp.bfloat16):
    array = scale * jax.random.normal(key, dims, jnp.float32)
    if pieces:
        array = array * shard_levels(key, dims, pieces, -0.22, 0.18)
    return jnp.clip(array, -reach, reach).astype(dtype)


def setup_inputs(seed: int = 0, part: int = 0) -> dict:
    keys = jax.random.split(jax.random.key(seed), 3)
    part_keys = jax.random.split(jax.random.fold_in(keys[2], part), 3)
    amplitudes = normal_values(part_keys[0], (2, AMPS), 1.0, 6.0, ((1, 16),), jnp.float32)
    gates = normal_values(keys[1], (2, GATES, GORDER, GORDER), (2 * GORDER) ** -0.5, 0.375, (), jnp.float32)
    return {"amplitudes": amplitudes, "gates": gates}


def apply_gate(state, gate_pair, offset):
    total = state.shape[1]
    inner = 1 << offset
    view = state.reshape(2, total // (128 * inner), 128, inner)
    real_in, imag_in = view[0], view[1]
    real_g, imag_g = gate_pair[0], gate_pair[1]
    hp = lax.Precision.HIGHEST
    real_out = jnp.einsum('ij,ajb->aib', real_g, real_in, precision=hp) - jnp.einsum('ij,ajb->aib', imag_g, imag_in, precision=hp)
    imag_out = jnp.einsum('ij,ajb->aib', real_g, imag_in, precision=hp) + jnp.einsum('ij,ajb->aib', imag_g, real_in, precision=hp)
    return jnp.stack([real_out, imag_out], 0).reshape(2, total)


def swap_bits(state, low, high):
    total = state.shape[1]
    view = state.reshape(2, total >> (high + 1), 2, (1 << high) >> (low + 1), 2, 1 << low)
    view = jnp.swapaxes(view, 2, 4)
    return view.reshape(2, total)


def run_section(state, gates, first, offsets):
    distinct = gates.shape[1]
    for step in range(4):
        state = apply_gate(state, gates[:, (first + step) % distinct], offsets[step])
    return state


def reference(amplitudes, gates):
    locq = int(LOC).bit_length() - 1
    globq = int(N_NODE).bit_length() - 1
    offsets = [0, (locq - 7) // 2, locq - 7, locq - 9]
    state = run_section(amplitudes, gates, 0, offsets)
    for k in range(3):
        state = swap_bits(state, locq - 1 - k, locq + k)
    state = run_section(state, gates, 4, offsets)
    count = 1 << globq
    total = state.shape[1]
    view = state.reshape(2, count, count, total // (count * count))
    state = jnp.swapaxes(view, 1, 2).reshape(2, total)
    return run_section(state, gates, 8, offsets)
```

```python
import functools

import jax
import jax.numpy as jnp
from jax import lax
from jax.experimental import pallas as pl
from jax.experimental.pallas import tpu as pltpu
from jax.sharding import PartitionSpec as P

F32, BF16 = jnp.float32, jnp.bfloat16
LANES = 128
NT = (((1,), (1,)), ((), ()))
NN = (((1,), (0,)), ((), ()))


def halves(x):
    high = x.astype(BF16)
    return high, (x - high.astype(F32)).astype(BF16)


def product(a, b, dims):
    (ah, al), (bh, bl) = a, b
    dot = functools.partial(lax.dot_general, dimension_numbers=dims, preferred_element_type=F32)
    return dot(ah, bh) + (dot(al, bh) + dot(ah, bl))


def natural_gate(g):
    return g[0], g[1]


def regrouped_gate(g):
    order = lax.broadcasted_iota(jnp.int32, (LANES, LANES), 1)
    order = (order % 16) * 8 + order // 16
    out = []
    for c in range(2):
        rows = jnp.concatenate([g[c, pl.ds(m, 16, stride=8), :] for m in range(8)], 0)
        out.append(jnp.take_along_axis(rows, order, axis=1))
    return out


def prepare(pair, mh, ml):
    re, im = pair
    for r, row in enumerate(((re, -im), (im, re))):
        for c, part in enumerate(row):
            high, low = halves(part)
            at = (pl.ds(r * LANES, LANES), pl.ds(c * LANES, LANES))
            mh[at] = high
            ml[at] = low


def right_gate(x_re, x_im, m):
    out = product(halves(jnp.concatenate([x_re, x_im], 1)), m, NT)
    return out[:, :LANES], out[:, LANES:]


def left_gate(x_re, x_im, m):
    out = product(m, halves(jnp.concatenate([x_re, x_im], 0)), NN)
    return out[:LANES], out[LANES:]


def exchange(blocks):
    blocks = list(blocks)
    lane = lax.broadcasted_iota(jnp.int32, blocks[0].shape, 1)
    for bit, shift in ((4, 64), (2, 32), (1, 16)):
        low = (lane & shift) == 0
        for k in range(8):
            if k & bit == 0:
                a, b = blocks[k], blocks[k | bit]
                blocks[k] = jnp.where(low, a, pltpu.roll(b, shift, 1))
                blocks[k | bit] = jnp.where(low, pltpu.roll(a, LANES - shift, 1), b)
    return blocks


def high_gate(s, m):
    for pair in range(2):
        bs = (2 * pair, 2 * pair + 1)
        x = [jnp.concatenate([s[c, pl.ds(b, LANES, stride=4), :] for b in bs], 1) for c in range(2)]
        y = left_gate(*x, m)
        for c in range(2):
            for k, b in enumerate(bs):
                s[c, pl.ds(b, LANES, stride=4), :] = y[c][:, k * LANES : (k + 1) * LANES]


def upper_gate(s, m, store):
    for pair in range(2):
        bs = (2 * pair, 2 * pair + 1)
        x = [jnp.concatenate([s[c, pl.ds(b * LANES, LANES), :] for b in bs], 1) for c in range(2)]
        y = left_gate(*x, m)
        for c in range(2):
            for k, b in enumerate(bs):
                store(c, b * LANES, y[c][:, k * LANES : (k + 1) * LANES])


def middle_gate(s, m):
    for pair in range(2):
        bs = (2 * pair, 2 * pair + 1)
        x = [
            jnp.concatenate(
                [
                    jnp.concatenate(exchange([s[c, pl.ds(b * LANES + 16 * k, 16), :] for k in range(8)]), 0)
                    for b in bs
                ],
                1,
            )
            for c in range(2)
        ]
        y = left_gate(*x, m)
        for c in range(2):
            for n, b in enumerate(bs):
                part = y[c][:, n * LANES : (n + 1) * LANES]
                back = exchange([part[16 * k : 16 * k + 16] for k in range(8)])
                s[c, pl.ds(b * LANES, LANES), :] = jnp.concatenate(back, 0)


def low_gate(s, m):
    for b in range(4):
        at = pl.ds(b * LANES, LANES)
        y = right_gate(s[0, at, :], s[1, at, :], m)
        for c in range(2):
            s[c, at, :] = y[c]


def fetch(gates, own, sems, indices):
    copies = []
    for slot, g in enumerate(indices):
        for c in range(2):
            copies.append(pltpu.make_async_copy(gates.at[c, g], own.at[slot, c], sems.at[slot, c]))
            copies[-1].start()
    return copies


def reversed3(v):
    return ((v & 1) << 2) | (v & 2) | ((v >> 2) & 1)


def first_kernel(indices, me_ref, amps, gates, keep, send, s, own, sems, mh, ml):
    copies = fetch(gates, own, sems, indices)
    low3 = me_ref[0] & 7

    def ready(slot, regroup=False):
        copies[2 * slot].wait()
        copies[2 * slot + 1].wait()
        g = own.at[slot]
        prepare(regrouped_gate(g) if regroup else natural_gate(g), mh.at[slot], ml.at[slot])
        return mh[slot], ml[slot]

    m = ready(0)
    for b in range(4):
        x = [amps[pl.ds(2 * LANES * b + c, LANES, stride=2), :] for c in range(2)]
        y = right_gate(*x, m)
        for c in range(2):
            s[c, pl.ds(b * LANES, LANES), :] = y[c]
    middle_gate(s, ready(1, True))
    high_gate(s, ready(2))

    def store(c, row, value):
        s[c, pl.ds(row, LANES), :] = value

    upper_gate(s, ready(3), store)
    low_gate(s, ready(4))
    middle_gate(s, ready(5, True))
    m = ready(6)
    for p in range(4):
        for core, out in ((0, keep), (1, send)):
            block = reversed3(low3 ^ (2 * p + core))
            at = pl.ds(pl.multiple_of(block * 64, 64), 64)
            y = right_gate(s[0, at, :], s[1, at, :], m)
            for c in range(2):
                out[p, c] = y[c]


def second_kernel(indices, me_ref, keep0, recv0, r1, r2, r3, gates, keep, send, s, own, sems, mh, ml):
    copies = fetch(gates, own, sems, indices)
    me = me_ref[0]
    low3 = me & 7
    parts = ((keep0, recv0), (r1, r1), (r2, r2), (r3, r3))
    for p in range(4):
        for core in range(2):
            block = reversed3(low3 ^ (2 * p + core))
            at = pl.ds(pl.multiple_of(block * 64, 64), 64)
            for c in range(2):
                s[c, at, :] = parts[p][core][c] if p == 0 else parts[p][core][core, c]

    def ready(slot, regroup=False):
        copies[2 * slot].wait()
        copies[2 * slot + 1].wait()
        g = own.at[slot]
        prepare(regrouped_gate(g) if regroup else natural_gate(g), mh.at[slot], ml.at[slot])
        return mh[slot], ml[slot]

    def store(c, row, value):
        s[c, pl.ds(row, LANES), :] = value

    high_gate(s, ready(0))
    upper_gate(s, ready(1), store)
    middle_gate(s, ready(2, True))
    for q in range(8):
        for core, out in ((0, keep), (1, send)):
            block = me ^ (2 * q + core)
            at = pl.ds(pl.multiple_of(block * 32, 32), 32)
            for c in range(2):
                out[q, c] = s[c, at, :]


def third_kernel(indices, me_ref, keep0, recv0, *rest):
    arrived, (gates, out, s, own, sems, mh, ml) = rest[:7], rest[7:]
    copies = fetch(gates, own, sems, indices)
    me = me_ref[0]
    for q in range(8):
        for core in range(2):
            block = me ^ (2 * q + core)
            at = pl.ds(pl.multiple_of(block * 32, 32), 32)
            for c in range(2):
                s[c, at, :] = (keep0, recv0)[core][c] if q == 0 else arrived[q - 1][core, c]

    def ready(slot):
        copies[2 * slot].wait()
        copies[2 * slot + 1].wait()
        prepare(natural_gate(own.at[slot]), mh.at[slot], ml.at[slot])
        return mh[slot], ml[slot]

    def store(c, row, value):
        out[pl.ds(2 * row + c, LANES, stride=2), :] = value

    high_gate(s, ready(0))
    upper_gate(s, ready(1), store)


def call(kernel, indices, outs, rows, operands, gates, me):
    n = len(indices)
    vmem = pl.BlockSpec(memory_space=pltpu.VMEM)
    return pl.pallas_call(
        functools.partial(kernel, indices),
        out_shape=outs,
        in_specs=[pl.BlockSpec(memory_space=pltpu.SMEM)] + [vmem] * len(operands) + [pl.BlockSpec(memory_space=pl.ANY)],
        out_specs=[vmem] * len(outs),
        scratch_shapes=[
            pltpu.VMEM((2, rows, LANES), F32),
            pltpu.VMEM((n, 2, LANES, LANES), F32),
            pltpu.SemaphoreType.DMA((n, 2)),
            pltpu.VMEM((n, 2 * LANES, 2 * LANES), BF16),
            pltpu.VMEM((n, 2 * LANES, 2 * LANES), BF16),
        ],
        compiler_params=pltpu.CompilerParams(vmem_limit_bytes=32 << 20),
    )(me, *operands, gates)


def flipped(block, mask):
    return lax.ppermute(block, "node", [(i, i ^ mask) for i in range(lax.axis_size("node"))])


def fast_body(amplitudes, gates):
    total = amplitudes.shape[1]
    rows = total // LANES
    shape = lambda *dims: jax.ShapeDtypeStruct(dims, F32)
    me = lax.axis_index("node").astype(jnp.int32).reshape(1)
    x = amplitudes.reshape(2, rows, LANES).transpose(1, 0, 2).reshape(2 * rows, LANES)
    half = shape(4, 2, rows // 8, LANES)
    keep, send = call(first_kernel, (0, 1, 2, 3, 4, 5, 8), [half, half], rows, [x], gates, me)
    recv = flipped(send, 1)
    far = [flipped(jnp.stack([keep[p], recv[p]]), 2 * p) for p in (3, 2, 1)]
    half = shape(8, 2, rows // 16, LANES)
    keep, send = call(
        second_kernel, (6, 7, 9), [half, half], rows, [keep[0], recv[0], far[2], far[1], far[0]], gates, me
    )
    recv = flipped(send, 1)
    far = {q: flipped(jnp.stack([keep[q], recv[q]]), 2 * q) for q in (6, 7, 4, 5, 2, 3, 1)}
    operands = [keep[0], recv[0]] + [far[q] for q in range(1, 8)]
    out = call(third_kernel, (10, 11), [shape(2 * rows, LANES)], rows, operands, gates, me)[0]
    return out.reshape(rows, 2, LANES).transpose(1, 0, 2).reshape(2, total)


def swapped(block, axis, apart):
    count = lax.axis_size(axis)
    route = []
    for low in range(count):
        high = low | 1 << apart
        if high != low and high < count:
            route += [(low, high), (high, low)]
    return lax.ppermute(block, axis, route)


def apply_gate(state, gate_pair, offset):
    total = state.shape[1]
    real_g, imag_g = (gate_pair[0], gate_pair[1])
    hp = lax.Precision.HIGHEST
    if offset == 0:
        view = state.reshape(2, total // 128, 128)
        real_in, imag_in = (view[0], view[1])
        real_out = jnp.einsum("ij,aj->ai", real_g, real_in, precision=hp) - jnp.einsum(
            "ij,aj->ai", imag_g, imag_in, precision=hp
        )
        imag_out = jnp.einsum("ij,aj->ai", real_g, imag_in, precision=hp) + jnp.einsum(
            "ij,aj->ai", imag_g, real_in, precision=hp
        )
        return jnp.stack([real_out, imag_out], 0).reshape(2, total)
    inner = 1 << offset
    outer = total // (128 * inner)
    folded = 1
    if inner < 128:
        folded = min(128 // inner, outer)
    view = state.reshape(2, outer // folded, folded, 128, inner)
    view = jnp.transpose(view, (0, 1, 3, 2, 4)).reshape(2, outer // folded, 128, folded * inner)
    real_in, imag_in = (view[0], view[1])
    real_out = jnp.einsum("ij,ajb->aib", real_g, real_in, precision=hp) - jnp.einsum(
        "ij,ajb->aib", imag_g, imag_in, precision=hp
    )
    imag_out = jnp.einsum("ij,ajb->aib", real_g, imag_in, precision=hp) + jnp.einsum(
        "ij,ajb->aib", imag_g, real_in, precision=hp
    )
    result = jnp.stack([real_out, imag_out], 0).reshape(2, outer // folded, 128, folded, inner)
    return jnp.transpose(result, (0, 1, 3, 2, 4)).reshape(2, total)


def run_gates(state, gates, indices, offsets):
    distinct = gates.shape[1]
    for index, offset in zip(indices, offsets):
        state = apply_gate(state, gates[:, index % distinct], offset)
    return state


def leave_alone(half):
    return half


def split_halves(state, position, bit):
    total = state.shape[1]
    mine = lax.axis_index("node") // (1 << bit) % 2
    view = state.reshape(2, total >> position + 1, 2, 1 << position)
    keep = lax.dynamic_index_in_dim(view, mine, 2, keepdims=False)
    other = lax.dynamic_index_in_dim(view, 1 - mine, 2, keepdims=False)
    return (mine, keep, other)


def join_halves(mine, keep, arrived, total):
    lower = jnp.where(mine == 0, keep, arrived)
    upper = jnp.where(mine == 0, arrived, keep)
    return jnp.stack([lower, upper], 2).reshape(2, total)


def enter_bit(state, position, bit, prepare):
    total = state.shape[1]
    mine, keep, other = split_halves(state, position, bit)
    other = prepare(other.reshape(2, total // 2)).reshape(keep.shape)
    arrived = swapped(other, "node", bit)
    keep = prepare(keep.reshape(2, total // 2)).reshape(arrived.shape)
    return join_halves(mine, keep, arrived, total)


def general_body(amplitudes, gates):
    total = amplitudes.shape[1]
    locq = total.bit_length() - 1
    devices_node = lax.axis_size("node")
    offsets = [0, (locq - 7) // 2, locq - 7, locq - 9]
    state = run_gates(amplitudes, gates, [0, 1, 2, 3], offsets)

    def early_gates(half):
        return run_gates(half, gates, [4, 5], offsets[:2])

    state = enter_bit(state, locq - 1, 0, early_gates)
    for bit in range(1, 3):
        state = enter_bit(state, locq - 1 - bit, bit, leave_alone)
    state = run_gates(state, gates, [6, 7], offsets[2:])
    blocks = state.reshape(2, devices_node, total // devices_node)
    blocks = lax.all_to_all(blocks, "node", split_axis=1, concat_axis=1, tiled=True)
    state = blocks.reshape(2, total)
    return run_gates(state, gates, [8, 9, 10, 11], offsets)


def body(amplitudes, gates):
    if amplitudes.shape[1] == 65536 and lax.axis_size("node") == 16 and gates.shape[1] == 12:
        return fast_body(amplitudes, gates)
    return general_body(amplitudes, gates)


def solution(mesh):
    in_specs = (P(None, ("paths", "node")), P())
    out_specs = P(None, ("paths", "node"))
    return jax.shard_map(body, mesh=mesh, in_specs=in_specs, out_specs=out_specs, check_vma=False)
```

```python
import functools

import jax
import jax.numpy as jnp
from jax import lax
from jax.experimental import pallas as pl
from jax.experimental.pallas import tpu as pltpu
from jax.sharding import PartitionSpec as P

F32, BF16 = jnp.float32, jnp.bfloat16
LANES = 128
PAIR = 2 * LANES
NT = (((1,), (1,)), ((), ()))
NN = (((1,), (0,)), ((), ()))
PORTS = (4, 2, 6)
VMEM = pl.BlockSpec(memory_space=pltpu.VMEM)
ANY = pl.BlockSpec(memory_space=pl.ANY)
HBM = pl.BlockSpec(memory_space=pltpu.HBM)


def halves(x):
    high = x.astype(BF16)
    return high, (x - high.astype(F32)).astype(BF16)


def product(a, b, dims):
    (ah, al), (bh, bl) = a, b
    dot = functools.partial(lax.dot_general, dimension_numbers=dims, preferred_element_type=F32)
    return dot(ah, bh) + (dot(al, bh) + dot(ah, bl))


def natural_gate(g):
    return g[0], g[1]


def regrouped_gate(g):
    order = lax.broadcasted_iota(jnp.int32, (LANES, LANES), 1)
    order = (order % 16) * 8 + order // 16
    out = []
    for c in range(2):
        rows = jnp.concatenate([g[c, pl.ds(m, 16, stride=8), :] for m in range(8)], 0)
        out.append(jnp.take_along_axis(rows, order, axis=1))
    return out


def prepare(g, regroup, mh, ml):
    re, im = regrouped_gate(g) if regroup else natural_gate(g)
    for r, row in enumerate(((re, -im), (im, re))):
        for c, part in enumerate(row):
            high, low = halves(part)
            at = (pl.ds(r * LANES, LANES), pl.ds(c * LANES, LANES))
            mh[at] = high
            ml[at] = low


def right_gate(x_re, x_im, m):
    out = product(halves(jnp.concatenate([x_re, x_im], 1)), m, NT)
    return out[:, :LANES], out[:, LANES:]


def left_gate(x_re, x_im, m):
    out = product(m, halves(jnp.concatenate([x_re, x_im], 0)), NN)
    return out[:LANES], out[LANES:]


def exchange(blocks):
    blocks = list(blocks)
    lane = lax.broadcasted_iota(jnp.int32, blocks[0].shape, 1)
    for bit, shift in ((4, 64), (2, 32), (1, 16)):
        low = (lane & shift) == 0
        for k in range(8):
            if k & bit == 0:
                a, b = blocks[k], blocks[k | bit]
                t = jnp.where(low, b, a)
                t = pltpu.roll(t, 64, 1) if shift == 64 else jnp.take_along_axis(t, lane ^ shift, axis=1)
                blocks[k] = jnp.where(low, a, t)
                blocks[k | bit] = jnp.where(low, t, b)
    return blocks


def high_gate(s, m):
    for pair in range(2):
        bs = (2 * pair, 2 * pair + 1)
        x = [jnp.concatenate([s[c, pl.ds(b, LANES, stride=4), :] for b in bs], 1) for c in range(2)]
        y = left_gate(*x, m)
        for c in range(2):
            for k, b in enumerate(bs):
                s[c, pl.ds(b, LANES, stride=4), :] = y[c][:, k * LANES : (k + 1) * LANES]


def upper_gate(s, m, store):
    for pair in range(2):
        bs = (2 * pair, 2 * pair + 1)
        x = [jnp.concatenate([s[c, pl.ds(b * LANES, LANES), :] for b in bs], 1) for c in range(2)]
        y = left_gate(*x, m)
        for c in range(2):
            for k, b in enumerate(bs):
                store(c, b * LANES, y[c][:, k * LANES : (k + 1) * LANES])


def middle_gate(s, m):
    count = s.shape[1] // LANES
    for first in range(0, count, 2):
        bs = tuple(range(first, min(first + 2, count)))
        x = [
            jnp.concatenate(
                [
                    jnp.concatenate(exchange([s[c, pl.ds(b * LANES + 16 * k, 16), :] for k in range(8)]), 0)
                    for b in bs
                ],
                1,
            )
            for c in range(2)
        ]
        y = left_gate(*x, m)
        for c in range(2):
            for n, b in enumerate(bs):
                part = y[c][:, n * LANES : (n + 1) * LANES]
                back = exchange([part[16 * k : 16 * k + 16] for k in range(8)])
                s[c, pl.ds(b * LANES, LANES), :] = jnp.concatenate(back, 0)


def low_gate(s, m):
    count = s.shape[1]
    for first in range(0, count, PAIR):
        at = pl.ds(first, min(PAIR, count - first))
        y = right_gate(s[0, at, :], s[1, at, :], m)
        for c in range(2):
            s[c, at, :] = y[c]


def keeper(s):
    def store(c, row, value):
        s[c, pl.ds(row, LANES), :] = value

    return store


def reversed3(v):
    return ((v & 1) << 2) | (v & 2) | ((v >> 2) & 1)


def rows_of(block, size):
    return pl.ds(pl.multiple_of(block * size, size), size)


def split(ref):
    return ref.at[0], ref.at[1]


class Gates:
    def __init__(self, source, scratch, indices):
        self.own, self.sems, self.mh, self.ml = scratch
        self.indices = indices
        self.copies = [
            pltpu.make_async_copy(source.at[:, g], self.own.at[k], self.sems.at[k]) for k, g in enumerate(indices)
        ]

    def start(self, ks):
        for k in ks:
            self.copies[k].start()

    def ready(self, ks):
        for k in ks:
            self.copies[k].wait()
        for k in ks:
            prepare(self.own.at[k], self.indices[k] % 4 == 1, self.mh.at[k], self.ml.at[k])

    def __getitem__(self, g):
        k = self.indices.index(g)
        return self.mh[k], self.ml[k]


def first_kernel(indices, me_ref, amps, gates, keep, send, s, own, sems, mh, ml, x, xsems):
    g = Gates(gates, (own, sems, mh, ml), indices)
    parts = []
    for b in range(2):
        at = pl.ds(2 * PAIR * b, 2 * PAIR)
        parts.append(pltpu.make_async_copy(amps.at[at], x.at[at], xsems.at[b]))
    g.start([0])
    for part in parts:
        part.start()
    g.start(range(1, len(indices)))
    low3 = me_ref[0] & 7
    g.ready([0])
    for b in range(2):
        parts[b].wait()
        y = right_gate(*[x[pl.ds(2 * PAIR * b + c, PAIR, stride=2), :] for c in range(2)], g[0])
        for c in range(2):
            s[c, pl.ds(b * PAIR, PAIR), :] = y[c]
    g.ready(range(1, len(indices)))
    middle_gate(s, g[1])
    high_gate(s, g[2])
    upper_gate(s, g[3], keeper(s))
    low_gate(s, g[4])
    middle_gate(s, g[5])
    for core, out in ((0, keep), (1, send)):
        ats = [rows_of(reversed3(low3 ^ (2 * p + core)), 64) for p in range(4)]
        y = right_gate(*[jnp.concatenate([s[c, at, :] for at in ats], 0) for c in range(2)], g[8])
        for p in range(4):
            for c in range(2):
                out[p, c] = y[c][64 * p : 64 * p + 64]


def second_kernel(indices, me_ref, keep0, recv0, r1, r2, r3, gates, own6, give, y1, self0, s, own, sems, mh, ml):
    g = Gates(gates, (own, sems, mh, ml), indices)
    g.start(range(3))
    me = me_ref[0]
    low3, core = me & 7, me & 1
    for p, part in enumerate(((keep0, recv0), split(r1), split(r2), split(r3))):
        for e in range(2):
            at = rows_of(reversed3(low3 ^ (2 * p + e)), 64)
            for c in range(2):
                s[c, at, :] = part[e][c]
    g.ready(range(3))
    high_gate(s, g[6])
    upper_gate(s, g[7], keeper(s))
    middle_gate(s, g[9])

    def write(out, first, mask, parts=(0, 1)):
        at = rows_of(me ^ mask, 32)
        for n, c in enumerate(parts):
            out[first + n] = s[c, at, :]

    for i, base in enumerate(PORTS):
        for f in range(2):
            write(own6.at[i, f], 0, 2 * (base + core) + f)
            write(give, 4 * i + 2 * f, 2 * (base + 1 - core) + (1 - f))
    write(give, 12, 3, (0,))
    write(give, 13, 1)
    write(y1, 0, 2)
    write(y1, 2, 3, (1,))
    write(self0, 0, 0)


def third_kernel(indices, me_ref, a0, a1, a2, y1, other, early, late, self0, gates, out, s, own, sems, mh, ml, y, ysems):
    g = Gates(gates, (own, sems, mh, ml), indices)
    g.start(range(2))
    me = me_ref[0]
    core = me & 1

    def place(part, first, mask, parts=(0, 1)):
        at = rows_of(me ^ mask, 32)
        for n, c in enumerate(parts):
            s[c, at, :] = part[first + n]

    for i, (base, arrived) in enumerate(zip(PORTS, (a0, a1, a2))):
        for src in range(2):
            place(arrived.at[0, src], 0, 2 * (base + core) + src)
            post, first = (early, 4 * i) if i < 2 else (late, 0)
            place(post, first + 2 * src, 2 * (base + 1 - core) + (1 - src))
    place(y1, 0, 2)
    place(y1, 3, 3, (0,))
    place(early, 8, 3, (1,))
    place(other, 0, 1)
    place(self0, 0, 0)
    g.ready(range(2))
    high_gate(s, g[10])
    copies = []

    def store(c, row, value):
        y[pl.ds(2 * row + c, LANES, stride=2), :] = value
        if c == 1 and row % PAIR == LANES:
            at = pl.ds(2 * (row - LANES), 2 * PAIR)
            copies.append(pltpu.make_async_copy(y.at[at], out.at[at], ysems.at[len(copies)]))
            copies[-1].start()

    upper_gate(s, g[11], store)
    for copy in copies:
        copy.wait()


def shape(*dims):
    return jax.ShapeDtypeStruct(dims, F32)


def call(kernel, indices, outs, rows, operands, specs, scratch=(), out_specs=None, limit=32 << 20):
    n = len(indices)
    return pl.pallas_call(
        functools.partial(kernel, indices),
        out_shape=outs,
        in_specs=[pl.BlockSpec(memory_space=pltpu.SMEM)] + specs,
        out_specs=out_specs or [VMEM] * len(outs),
        scratch_shapes=[
            pltpu.VMEM((2, rows, LANES), F32),
            pltpu.VMEM((n, 2, LANES, LANES), F32),
            pltpu.SemaphoreType.DMA((n,)),
            pltpu.VMEM((n, PAIR, PAIR), BF16),
            pltpu.VMEM((n, PAIR, PAIR), BF16),
            *scratch,
        ],
        compiler_params=pltpu.CompilerParams(vmem_limit_bytes=limit),
        name=kernel.__name__,
    )(*operands)


def flipped(block, mask, port=0):
    route = [(i, i ^ mask ^ (port if i & 1 else 0)) for i in range(lax.axis_size("node"))]
    return lax.ppermute(block, "node", route)


def fast_body(amplitudes, gates):
    total = amplitudes.shape[1]
    rows = total // LANES
    eighth, part16 = rows // 8, rows // 16
    me = lax.axis_index("node").astype(jnp.int32).reshape(1)
    x = amplitudes.reshape(2, rows, LANES).transpose(1, 0, 2).reshape(2 * rows, LANES)
    interleaved = (pltpu.VMEM((2 * rows, LANES), F32), pltpu.SemaphoreType.DMA((2,)))
    half = shape(4, 2, eighth, LANES)
    keep, send = call(
        first_kernel, (0, 1, 2, 3, 4, 5, 8), [half] * 2, rows, [me, x, gates], [HBM] * 2, interleaved, limit=532 * 104858
    )
    recv = flipped(send, 1)
    far = [flipped(jnp.stack([keep[p], recv[p]]), 2 * p) for p in (1, 2, 3)]
    block = (part16, LANES)
    own, give, y1, self0 = call(
        second_kernel,
        (6, 7, 9),
        [shape(3, 2, 2, *block), shape(15, *block), shape(3, *block), shape(2, *block)],
        rows,
        [me, keep[0], recv[0], *far, gates],
        [VMEM] * 5 + [HBM],
    )
    recv = flipped(give, 1)
    arrived = [
        flipped(jnp.stack([own[i], recv[4 * i : 4 * i + 4].reshape(2, 2, *block)], 1), 2 * base, 2)
        for i, base in enumerate(PORTS)
    ]
    y1 = flipped(jnp.concatenate([y1, recv[12:13]]), 2)
    early = [a[1].reshape(4, *block) for a in arrived]
    late = flipped(early[2], 1)
    early = flipped(jnp.concatenate(early[:2] + [y1[2:3]]), 1)
    out = call(
        third_kernel,
        (10, 11),
        [shape(2 * rows, LANES)],
        rows,
        [me, *arrived, y1, recv[13:], early, late, self0, gates],
        [VMEM] * 8 + [HBM],
        interleaved,
        [HBM],
    )[0]
    return out.reshape(rows, 2, LANES).transpose(1, 0, 2).reshape(2, total)


def swapped(block, axis, apart):
    count = lax.axis_size(axis)
    route = []
    for low in range(count):
        high = low | 1 << apart
        if high != low and high < count:
            route += [(low, high), (high, low)]
    return lax.ppermute(block, axis, route)


def apply_gate(state, gate_pair, offset):
    total = state.shape[1]
    real_g, imag_g = (gate_pair[0], gate_pair[1])
    hp = lax.Precision.HIGHEST
    if offset == 0:
        view = state.reshape(2, total // 128, 128)
        real_in, imag_in = (view[0], view[1])
        real_out = jnp.einsum("ij,aj->ai", real_g, real_in, precision=hp) - jnp.einsum(
            "ij,aj->ai", imag_g, imag_in, precision=hp
        )
        imag_out = jnp.einsum("ij,aj->ai", real_g, imag_in, precision=hp) + jnp.einsum(
            "ij,aj->ai", imag_g, real_in, precision=hp
        )
        return jnp.stack([real_out, imag_out], 0).reshape(2, total)
    inner = 1 << offset
    outer = total // (128 * inner)
    folded = 1
    if inner < 128:
        folded = min(128 // inner, outer)
    view = state.reshape(2, outer // folded, folded, 128, inner)
    view = jnp.transpose(view, (0, 1, 3, 2, 4)).reshape(2, outer // folded, 128, folded * inner)
    real_in, imag_in = (view[0], view[1])
    real_out = jnp.einsum("ij,ajb->aib", real_g, real_in, precision=hp) - jnp.einsum(
        "ij,ajb->aib", imag_g, imag_in, precision=hp
    )
    imag_out = jnp.einsum("ij,ajb->aib", real_g, imag_in, precision=hp) + jnp.einsum(
        "ij,ajb->aib", imag_g, real_in, precision=hp
    )
    result = jnp.stack([real_out, imag_out], 0).reshape(2, outer // folded, 128, folded, inner)
    return jnp.transpose(result, (0, 1, 3, 2, 4)).reshape(2, total)


def run_gates(state, gates, indices, offsets):
    distinct = gates.shape[1]
    for index, offset in zip(indices, offsets):
        state = apply_gate(state, gates[:, index % distinct], offset)
    return state


def leave_alone(half):
    return half


def split_halves(state, position, bit):
    total = state.shape[1]
    mine = lax.axis_index("node") // (1 << bit) % 2
    view = state.reshape(2, total >> position + 1, 2, 1 << position)
    keep = lax.dynamic_index_in_dim(view, mine, 2, keepdims=False)
    other = lax.dynamic_index_in_dim(view, 1 - mine, 2, keepdims=False)
    return (mine, keep, other)


def join_halves(mine, keep, arrived, total):
    lower = jnp.where(mine == 0, keep, arrived)
    upper = jnp.where(mine == 0, arrived, keep)
    return jnp.stack([lower, upper], 2).reshape(2, total)


def enter_bit(state, position, bit, prepare):
    total = state.shape[1]
    mine, keep, other = split_halves(state, position, bit)
    other = prepare(other.reshape(2, total // 2)).reshape(keep.shape)
    arrived = swapped(other, "node", bit)
    keep = prepare(keep.reshape(2, total // 2)).reshape(arrived.shape)
    return join_halves(mine, keep, arrived, total)


def general_body(amplitudes, gates):
    total = amplitudes.shape[1]
    locq = total.bit_length() - 1
    devices_node = lax.axis_size("node")
    offsets = [0, (locq - 7) // 2, locq - 7, locq - 9]
    state = run_gates(amplitudes, gates, [0, 1, 2, 3], offsets)

    def early_gates(half):
        return run_gates(half, gates, [4, 5], offsets[:2])

    state = enter_bit(state, locq - 1, 0, early_gates)
    for bit in range(1, 3):
        state = enter_bit(state, locq - 1 - bit, bit, leave_alone)
    state = run_gates(state, gates, [6, 7], offsets[2:])
    blocks = state.reshape(2, devices_node, total // devices_node)
    blocks = lax.all_to_all(blocks, "node", split_axis=1, concat_axis=1, tiled=True)
    state = blocks.reshape(2, total)
    return run_gates(state, gates, [8, 9, 10, 11], offsets)


def body(amplitudes, gates):
    if amplitudes.shape[1] == 65536 and lax.axis_size("node") == 16 and gates.shape[1] == 12:
        return fast_body(amplitudes, gates)
    return general_body(amplitudes, gates)


def solution(mesh):
    in_specs = (P(None, ("paths", "node")), P())
    out_specs = P(None, ("paths", "node"))
    return jax.shard_map(body, mesh=mesh, in_specs=in_specs, out_specs=out_specs, check_vma=False)
```

```python
import functools

import jax
import jax.numpy as jnp
from jax import lax
from jax.experimental import pallas as pl
from jax.experimental.pallas import tpu as pltpu
from jax.sharding import PartitionSpec as P

F32, BF16 = jnp.float32, jnp.bfloat16
LANES = 128
PAIR = 2 * LANES
NT = (((1,), (1,)), ((), ()))
NN = (((1,), (0,)), ((), ()))
PORTS = (4, 2, 6)
VMEM = pl.BlockSpec(memory_space=pltpu.VMEM)
ANY = pl.BlockSpec(memory_space=pl.ANY)
HBM = pl.BlockSpec(memory_space=pltpu.HBM)


def halves(x):
    high = x.astype(BF16)
    return high, (x - high.astype(F32)).astype(BF16)


def product(a, b, dims):
    (ah, al), (bh, bl) = a, b
    dot = functools.partial(lax.dot_general, dimension_numbers=dims, preferred_element_type=F32)
    return dot(ah, bh) + (dot(al, bh) + dot(ah, bl))


def natural_gate(g):
    return g[0], g[1]


def regrouped_gate(g):
    order = lax.broadcasted_iota(jnp.int32, (LANES, LANES), 1)
    order = (order % 16) * 8 + order // 16
    out = []
    for c in range(2):
        rows = jnp.concatenate([g[c, pl.ds(m, 16, stride=8), :] for m in range(8)], 0)
        out.append(jnp.take_along_axis(rows, order, axis=1))
    return out


def prepare(g, regroup, mh, ml):
    re, im = regrouped_gate(g) if regroup else natural_gate(g)
    for r, row in enumerate(((re, -im), (im, re))):
        for c, part in enumerate(row):
            high, low = halves(part)
            at = (pl.ds(r * LANES, LANES), pl.ds(c * LANES, LANES))
            mh[at] = high
            ml[at] = low


def right_gate(x_re, x_im, m):
    out = product(halves(jnp.concatenate([x_re, x_im], 1)), m, NT)
    return out[:, :LANES], out[:, LANES:]


def left_gate(x_re, x_im, m):
    out = product(m, halves(jnp.concatenate([x_re, x_im], 0)), NN)
    return out[:LANES], out[LANES:]


def exchange(blocks):
    blocks = list(blocks)
    lane = lax.broadcasted_iota(jnp.int32, blocks[0].shape, 1)
    for bit, shift in ((4, 64), (2, 32), (1, 16)):
        low = (lane & shift) == 0
        for k in range(8):
            if k & bit == 0:
                a, b = blocks[k], blocks[k | bit]
                t = jnp.where(low, b, a)
                t = pltpu.roll(t, 64, 1) if shift == 64 else jnp.take_along_axis(t, lane ^ shift, axis=1)
                blocks[k] = jnp.where(low, a, t)
                blocks[k | bit] = jnp.where(low, t, b)
    return blocks


def high_gate(s, m):
    for pair in range(2):
        bs = (2 * pair, 2 * pair + 1)
        x = [jnp.concatenate([s[c, pl.ds(b, LANES, stride=4), :] for b in bs], 1) for c in range(2)]
        y = left_gate(*x, m)
        for c in range(2):
            for k, b in enumerate(bs):
                s[c, pl.ds(b, LANES, stride=4), :] = y[c][:, k * LANES : (k + 1) * LANES]


def upper_gate(s, m, store):
    for pair in range(2):
        bs = (2 * pair, 2 * pair + 1)
        x = [jnp.concatenate([s[c, pl.ds(b * LANES, LANES), :] for b in bs], 1) for c in range(2)]
        y = left_gate(*x, m)
        for c in range(2):
            for k, b in enumerate(bs):
                store(c, b * LANES, y[c][:, k * LANES : (k + 1) * LANES])


def middle_gate(s, m):
    count = s.shape[1] // LANES
    for first in range(0, count, 2):
        bs = tuple(range(first, min(first + 2, count)))
        x = [
            jnp.concatenate(
                [
                    jnp.concatenate(exchange([s[c, pl.ds(b * LANES + 16 * k, 16), :] for k in range(8)]), 0)
                    for b in bs
                ],
                1,
            )
            for c in range(2)
        ]
        y = left_gate(*x, m)
        for c in range(2):
            for n, b in enumerate(bs):
                part = y[c][:, n * LANES : (n + 1) * LANES]
                back = exchange([part[16 * k : 16 * k + 16] for k in range(8)])
                s[c, pl.ds(b * LANES, LANES), :] = jnp.concatenate(back, 0)


def low_gate(s, m):
    count = s.shape[1]
    for first in range(0, count, PAIR):
        at = pl.ds(first, min(PAIR, count - first))
        y = right_gate(s[0, at, :], s[1, at, :], m)
        for c in range(2):
            s[c, at, :] = y[c]


def keeper(s):
    def store(c, row, value):
        s[c, pl.ds(row, LANES), :] = value

    return store


def reversed3(v):
    return ((v & 1) << 2) | (v & 2) | ((v >> 2) & 1)


def rows_of(block, size):
    return pl.ds(pl.multiple_of(block * size, size), size)


def split(ref):
    return ref.at[0], ref.at[1]


class Gates:
    def __init__(self, source, scratch, indices):
        self.own, self.sems, self.mh, self.ml = scratch
        self.indices = indices
        self.copies = [
            pltpu.make_async_copy(source.at[:, g], self.own.at[k], self.sems.at[k]) for k, g in enumerate(indices)
        ]

    def start(self, ks):
        for k in ks:
            self.copies[k].start()

    def ready(self, ks):
        for k in ks:
            self.copies[k].wait()
        for k in ks:
            prepare(self.own.at[k], self.indices[k] % 4 == 1, self.mh.at[k], self.ml.at[k])

    def __getitem__(self, g):
        k = self.indices.index(g)
        return self.mh[k], self.ml[k]


class Ready:
    def __init__(self, source, scratch, indices):
        self.mh, self.ml = scratch
        self.indices = indices
        for k, g in enumerate(indices):
            prepare(source.at[:, g], g % 4 == 1, self.mh.at[k], self.ml.at[k])

    def __getitem__(self, g):
        k = self.indices.index(g)
        return self.mh[k], self.ml[k]


def first_kernel(indices, me_ref, amps, gates, q1, q2, own3, own0, give, s, own, sems, mh, ml, x, xsems):
    g = Gates(gates, (own, sems, mh, ml), indices)
    parts = []
    for b in range(2):
        at = pl.ds(2 * PAIR * b, 2 * PAIR)
        parts.append(pltpu.make_async_copy(amps.at[at], x.at[at], xsems.at[b]))
    g.start([0])
    for part in parts:
        part.start()
    g.start(range(1, len(indices)))
    low3 = me_ref[0] & 7
    g.ready([0])
    for b in range(2):
        parts[b].wait()
        y = right_gate(*[x[pl.ds(2 * PAIR * b + c, PAIR, stride=2), :] for c in range(2)], g[0])
        for c in range(2):
            s[c, pl.ds(b * PAIR, PAIR), :] = y[c]
    g.ready(range(1, len(indices)))
    middle_gate(s, g[1])
    high_gate(s, g[2])
    upper_gate(s, g[3], keeper(s))
    low_gate(s, g[4])
    middle_gate(s, g[5])
    outs = ((own0, give.at[0]), split(q1), split(q2), (own3, give.at[1]))
    for e in range(2):
        ats = [rows_of(reversed3(low3 ^ (2 * p + e)), 64) for p in range(4)]
        y = right_gate(*[jnp.concatenate([s[c, at, :] for at in ats], 0) for c in range(2)], g[8])
        for p in range(4):
            for c in range(2):
                outs[p][e][c] = y[c][64 * p : 64 * p + 64]


def second_kernel(indices, me_ref, own0, other0, r1, r2, r3, post1, post2, gates, own6, give, y1, self0, s, mh, ml):
    g = Ready(gates, (mh, ml), indices)
    me = me_ref[0]
    low3, core = me & 7, me & 1
    for mask, part in enumerate((own0, other0, r1.at[0], post1, r2.at[0], post2, r3.at[0], r3.at[1])):
        at = rows_of(reversed3(low3 ^ mask), 64)
        for c in range(2):
            s[c, at, :] = part[c]
    high_gate(s, g[6])
    upper_gate(s, g[7], keeper(s))
    middle_gate(s, g[9])

    def write(out, first, mask, parts=(0, 1)):
        at = rows_of(me ^ mask, 32)
        for n, c in enumerate(parts):
            out[first + n] = s[c, at, :]

    for i, base in enumerate(PORTS):
        for f in range(2):
            write(own6.at[i, f], 0, 2 * (base + core) + f)
            write(give, 4 * i + 2 * f, 2 * (base + 1 - core) + (1 - f))
    write(give, 12, 3, (0,))
    write(give, 13, 1)
    write(y1, 0, 2)
    write(y1, 2, 3, (1,))
    write(self0, 0, 0)


def third_kernel(indices, me_ref, a0, a1, a2, y1, other, early, late, self0, gates, out, s, mh, ml, y, ysems):
    g = Ready(gates, (mh, ml), indices)
    me = me_ref[0]
    core = me & 1

    def place(part, first, mask, parts=(0, 1)):
        at = rows_of(me ^ mask, 32)
        for n, c in enumerate(parts):
            s[c, at, :] = part[first + n]

    for i, (base, arrived) in enumerate(zip(PORTS, (a0, a1, a2))):
        for src in range(2):
            place(arrived.at[0, src], 0, 2 * (base + core) + src)
            post, first = (early, 4 * i) if i < 2 else (late, 0)
            place(post, first + 2 * src, 2 * (base + 1 - core) + (1 - src))
    place(y1, 0, 2)
    place(y1, 3, 3, (0,))
    place(early, 8, 3, (1,))
    place(other, 0, 1)
    place(self0, 0, 0)
    high_gate(s, g[10])
    copies = []

    def store(c, row, value):
        y[pl.ds(2 * row + c, LANES, stride=2), :] = value
        if c == 1 and row % PAIR == LANES:
            at = pl.ds(2 * (row - LANES), 2 * PAIR)
            copies.append(pltpu.make_async_copy(y.at[at], out.at[at], ysems.at[len(copies)]))
            copies[-1].start()

    upper_gate(s, g[11], store)
    for copy in copies:
        copy.wait()


def shape(*dims):
    return jax.ShapeDtypeStruct(dims, F32)


def call(kernel, indices, outs, rows, operands, specs, scratch=(), out_specs=None, limit=32 << 20):
    n = len(indices)
    fetch = [pltpu.VMEM((n, 2, LANES, LANES), F32), pltpu.SemaphoreType.DMA((n,))] if specs[-1] is HBM else []
    return pl.pallas_call(
        functools.partial(kernel, indices),
        out_shape=outs,
        in_specs=[pl.BlockSpec(memory_space=pltpu.SMEM)] + specs,
        out_specs=out_specs or [VMEM] * len(outs),
        scratch_shapes=[
            pltpu.VMEM((2, rows, LANES), F32),
            *fetch,
            pltpu.VMEM((n, PAIR, PAIR), BF16),
            pltpu.VMEM((n, PAIR, PAIR), BF16),
            *scratch,
        ],
        compiler_params=pltpu.CompilerParams(vmem_limit_bytes=limit),
        name=kernel.__name__,
    )(*operands)


def flipped(block, mask, port=0):
    route = [(i, i ^ mask ^ (port if i & 1 else 0)) for i in range(lax.axis_size("node"))]
    return lax.ppermute(block, "node", route)


def fast_body(amplitudes, gates):
    total = amplitudes.shape[1]
    rows = total // LANES
    eighth, part16 = rows // 8, rows // 16
    me = lax.axis_index("node").astype(jnp.int32).reshape(1)
    x = amplitudes.reshape(2, rows, LANES).transpose(1, 0, 2).reshape(2 * rows, LANES)
    interleaved = (pltpu.VMEM((2 * rows, LANES), F32), pltpu.SemaphoreType.DMA((2,)))
    one, two = shape(2, eighth, LANES), shape(2, 2, eighth, LANES)
    q1, q2, own3, own0, give = call(
        first_kernel,
        (0, 1, 2, 3, 4, 5, 8),
        [two, two, one, one, two],
        rows,
        [me, x, gates],
        [HBM] * 2,
        interleaved,
        limit=532 * 104858,
    )
    recv = flipped(give, 1)
    r1, r2 = flipped(q1, 2), flipped(q2, 4)
    r3 = flipped(jnp.stack([own3, recv[1]]), 6)
    post1, post2 = flipped(r1[1], 1), flipped(r2[1], 1)
    block = (part16, LANES)
    own, give, y1, self0 = call(
        second_kernel,
        (6, 7, 9),
        [shape(3, 2, 2, *block), shape(15, *block), shape(3, *block), shape(2, *block)],
        rows,
        [me, own0, recv[0], r1, r2, r3, post1, post2, gates],
        [VMEM] * 8,
    )
    recv = flipped(give, 1)
    arrived = [
        flipped(jnp.stack([own[i], recv[4 * i : 4 * i + 4].reshape(2, 2, *block)], 1), 2 * base, 2)
        for i, base in enumerate(PORTS)
    ]
    y1 = flipped(jnp.concatenate([y1, recv[12:13]]), 2)
    early = [a[1].reshape(4, *block) for a in arrived]
    late = flipped(early[2], 1)
    early = flipped(jnp.concatenate(early[:2] + [y1[2:3]]), 1)
    out = call(
        third_kernel,
        (10, 11),
        [shape(2 * rows, LANES)],
        rows,
        [me, *arrived, y1, recv[13:], early, late, self0, gates],
        [VMEM] * 9,
        interleaved,
        [HBM],
    )[0]
    return out.reshape(rows, 2, LANES).transpose(1, 0, 2).reshape(2, total)


def swapped(block, axis, apart):
    count = lax.axis_size(axis)
    route = []
    for low in range(count):
        high = low | 1 << apart
        if high != low and high < count:
            route += [(low, high), (high, low)]
    return lax.ppermute(block, axis, route)


def apply_gate(state, gate_pair, offset):
    total = state.shape[1]
    real_g, imag_g = (gate_pair[0], gate_pair[1])
    hp = lax.Precision.HIGHEST
    if offset == 0:
        view = state.reshape(2, total // 128, 128)
        real_in, imag_in = (view[0], view[1])
        real_out = jnp.einsum("ij,aj->ai", real_g, real_in, precision=hp) - jnp.einsum(
            "ij,aj->ai", imag_g, imag_in, precision=hp
        )
        imag_out = jnp.einsum("ij,aj->ai", real_g, imag_in, precision=hp) + jnp.einsum(
            "ij,aj->ai", imag_g, real_in, precision=hp
        )
        return jnp.stack([real_out, imag_out], 0).reshape(2, total)
    inner = 1 << offset
    outer = total // (128 * inner)
    folded = 1
    if inner < 128:
        folded = min(128 // inner, outer)
    view = state.reshape(2, outer // folded, folded, 128, inner)
    view = jnp.transpose(view, (0, 1, 3, 2, 4)).reshape(2, outer // folded, 128, folded * inner)
    real_in, imag_in = (view[0], view[1])
    real_out = jnp.einsum("ij,ajb->aib", real_g, real_in, precision=hp) - jnp.einsum(
        "ij,ajb->aib", imag_g, imag_in, precision=hp
    )
    imag_out = jnp.einsum("ij,ajb->aib", real_g, imag_in, precision=hp) + jnp.einsum(
        "ij,ajb->aib", imag_g, real_in, precision=hp
    )
    result = jnp.stack([real_out, imag_out], 0).reshape(2, outer // folded, 128, folded, inner)
    return jnp.transpose(result, (0, 1, 3, 2, 4)).reshape(2, total)


def run_gates(state, gates, indices, offsets):
    distinct = gates.shape[1]
    for index, offset in zip(indices, offsets):
        state = apply_gate(state, gates[:, index % distinct], offset)
    return state


def leave_alone(half):
    return half


def split_halves(state, position, bit):
    total = state.shape[1]
    mine = lax.axis_index("node") // (1 << bit) % 2
    view = state.reshape(2, total >> position + 1, 2, 1 << position)
    keep = lax.dynamic_index_in_dim(view, mine, 2, keepdims=False)
    other = lax.dynamic_index_in_dim(view, 1 - mine, 2, keepdims=False)
    return (mine, keep, other)


def join_halves(mine, keep, arrived, total):
    lower = jnp.where(mine == 0, keep, arrived)
    upper = jnp.where(mine == 0, arrived, keep)
    return jnp.stack([lower, upper], 2).reshape(2, total)


def enter_bit(state, position, bit, prepare):
    total = state.shape[1]
    mine, keep, other = split_halves(state, position, bit)
    other = prepare(other.reshape(2, total // 2)).reshape(keep.shape)
    arrived = swapped(other, "node", bit)
    keep = prepare(keep.reshape(2, total // 2)).reshape(arrived.shape)
    return join_halves(mine, keep, arrived, total)


def general_body(amplitudes, gates):
    total = amplitudes.shape[1]
    locq = total.bit_length() - 1
    devices_node = lax.axis_size("node")
    offsets = [0, (locq - 7) // 2, locq - 7, locq - 9]
    state = run_gates(amplitudes, gates, [0, 1, 2, 3], offsets)

    def early_gates(half):
        return run_gates(half, gates, [4, 5], offsets[:2])

    state = enter_bit(state, locq - 1, 0, early_gates)
    for bit in range(1, 3):
        state = enter_bit(state, locq - 1 - bit, bit, leave_alone)
    state = run_gates(state, gates, [6, 7], offsets[2:])
    blocks = state.reshape(2, devices_node, total // devices_node)
    blocks = lax.all_to_all(blocks, "node", split_axis=1, concat_axis=1, tiled=True)
    state = blocks.reshape(2, total)
    return run_gates(state, gates, [8, 9, 10, 11], offsets)


def body(amplitudes, gates):
    if amplitudes.shape[1] == 65536 and lax.axis_size("node") == 16 and gates.shape[1] == 12:
        return fast_body(amplitudes, gates)
    return general_body(amplitudes, gates)


def solution(mesh):
    in_specs = (P(None, ("paths", "node")), P())
    out_specs = P(None, ("paths", "node"))
    return jax.shard_map(body, mesh=mesh, in_specs=in_specs, out_specs=out_specs, check_vma=False)
```

```python
import functools

import jax
import jax.numpy as jnp
from jax import lax
from jax.experimental import pallas as pl
from jax.experimental.pallas import tpu as pltpu
from jax.sharding import PartitionSpec as P

F32, BF16 = jnp.float32, jnp.bfloat16
LANES = 128
PAIR = 2 * LANES
NT = (((1,), (1,)), ((), ()))
NN = (((1,), (0,)), ((), ()))
PORTS = (4, 2, 6)
SMEM = pl.BlockSpec(memory_space=pltpu.SMEM)
VMEM = pl.BlockSpec(memory_space=pltpu.VMEM)
ANY = pl.BlockSpec(memory_space=pl.ANY)
HBM = pl.BlockSpec(memory_space=pltpu.HBM)


def halves(x):
    high = x.astype(BF16)
    return high, (x - high.astype(F32)).astype(BF16)


def product(a, b, dims):
    (ah, al), (bh, bl) = a, b
    dot = functools.partial(lax.dot_general, dimension_numbers=dims, preferred_element_type=F32)
    return dot(ah, bh) + (dot(al, bh) + dot(ah, bl))


def natural_gate(g):
    return g[0], g[1]


def regrouped_gate(g):
    order = lax.broadcasted_iota(jnp.int32, (LANES, LANES), 1)
    order = (order % 16) * 8 + order // 16
    out = []
    for c in range(2):
        rows = jnp.concatenate([g[c, pl.ds(m, 16, stride=8), :] for m in range(8)], 0)
        out.append(jnp.take_along_axis(rows, order, axis=1))
    return out


def prepare(g, regroup, mh, ml):
    re, im = regrouped_gate(g) if regroup else natural_gate(g)
    for r, row in enumerate(((re, -im), (im, re))):
        for c, part in enumerate(row):
            high, low = halves(part)
            at = (pl.ds(r * LANES, LANES), pl.ds(c * LANES, LANES))
            mh[at] = high
            ml[at] = low


def right_gate(x_re, x_im, m):
    out = product(halves(jnp.concatenate([x_re, x_im], 1)), m, NT)
    return out[:, :LANES], out[:, LANES:]


def left_gate(x_re, x_im, m):
    out = product(m, halves(jnp.concatenate([x_re, x_im], 0)), NN)
    return out[:LANES], out[LANES:]


def exchange(blocks):
    blocks = list(blocks)
    lane = lax.broadcasted_iota(jnp.int32, blocks[0].shape, 1)
    for bit, shift in ((4, 64), (2, 32), (1, 16)):
        low = (lane & shift) == 0
        for k in range(8):
            if k & bit == 0:
                a, b = blocks[k], blocks[k | bit]
                t = jnp.where(low, b, a)
                t = pltpu.roll(t, 64, 1) if shift == 64 else jnp.take_along_axis(t, lane ^ shift, axis=1)
                blocks[k] = jnp.where(low, a, t)
                blocks[k | bit] = jnp.where(low, t, b)
    return blocks


def high_gate(s, m):
    for pair in range(2):
        bs = (2 * pair, 2 * pair + 1)
        x = [jnp.concatenate([s[c, pl.ds(b, LANES, stride=4), :] for b in bs], 1) for c in range(2)]
        y = left_gate(*x, m)
        for c in range(2):
            for k, b in enumerate(bs):
                s[c, pl.ds(b, LANES, stride=4), :] = y[c][:, k * LANES : (k + 1) * LANES]


def upper_gate(s, m, store):
    for pair in range(2):
        bs = (2 * pair, 2 * pair + 1)
        x = [jnp.concatenate([s[c, pl.ds(b * LANES, LANES), :] for b in bs], 1) for c in range(2)]
        y = left_gate(*x, m)
        for c in range(2):
            for k, b in enumerate(bs):
                store(c, b * LANES, y[c][:, k * LANES : (k + 1) * LANES])


def middle_gate(s, m):
    count = s.shape[1] // LANES
    for first in range(0, count, 2):
        bs = tuple(range(first, min(first + 2, count)))
        x = [
            jnp.concatenate(
                [
                    jnp.concatenate(exchange([s[c, pl.ds(b * LANES + 16 * k, 16), :] for k in range(8)]), 0)
                    for b in bs
                ],
                1,
            )
            for c in range(2)
        ]
        y = left_gate(*x, m)
        for c in range(2):
            for n, b in enumerate(bs):
                part = y[c][:, n * LANES : (n + 1) * LANES]
                back = exchange([part[16 * k : 16 * k + 16] for k in range(8)])
                s[c, pl.ds(b * LANES, LANES), :] = jnp.concatenate(back, 0)


def low_gate(s, m):
    count = s.shape[1]
    for first in range(0, count, PAIR):
        at = pl.ds(first, min(PAIR, count - first))
        y = right_gate(s[0, at, :], s[1, at, :], m)
        for c in range(2):
            s[c, at, :] = y[c]


def keeper(s):
    def store(c, row, value):
        s[c, pl.ds(row, LANES), :] = value

    return store


def reversed3(v):
    return ((v & 1) << 2) | (v & 2) | ((v >> 2) & 1)


def rows_of(block, size):
    return pl.ds(pl.multiple_of(block * size, size), size)


def split(ref):
    return ref.at[0], ref.at[1]


class Gates:
    def __init__(self, source, scratch, indices):
        self.own, self.sems, self.mh, self.ml = scratch
        self.indices = indices
        self.copies = [
            pltpu.make_async_copy(source.at[:, g], self.own.at[k], self.sems.at[k]) for k, g in enumerate(indices)
        ]

    def start(self, ks):
        for k in ks:
            self.copies[k].start()

    def ready(self, ks):
        for k in ks:
            self.copies[k].wait()
        for k in ks:
            prepare(self.own.at[k], self.indices[k] % 4 == 1, self.mh.at[k], self.ml.at[k])

    def __getitem__(self, g):
        k = self.indices.index(g)
        return self.mh[k], self.ml[k]


class Ready:
    def __init__(self, source, scratch, indices):
        self.mh, self.ml = scratch
        self.indices = indices
        for k, g in enumerate(indices):
            prepare(source.at[:, g], g % 4 == 1, self.mh.at[k], self.ml.at[k])

    def __getitem__(self, g):
        k = self.indices.index(g)
        return self.mh[k], self.ml[k]


def lower_gates(s, g):
    low_gate(s, g[4])
    middle_gate(s, g[5])
    low_gate(s, g[8])


def first_kernel(indices, me_ref, amps, gates, q1, q2, own3, own0, give, s, own, sems, mh, ml, x, xsems, part):
    g = Gates(gates, (own, sems, mh, ml), indices)
    parts = []
    for b in range(2):
        at = pl.ds(2 * PAIR * b, 2 * PAIR)
        parts.append(pltpu.make_async_copy(amps.at[at], x.at[at], xsems.at[b]))
    g.start([0])
    for copy in parts:
        copy.start()
    g.start(range(1, len(indices)))
    low3 = me_ref[0] & 7
    g.ready([0])
    for b in range(2):
        parts[b].wait()
        y = right_gate(*[x[pl.ds(2 * PAIR * b + c, PAIR, stride=2), :] for c in range(2)], g[0])
        for c in range(2):
            s[c, pl.ds(b * PAIR, PAIR), :] = y[c]
    g.ready(range(1, len(indices)))
    middle_gate(s, g[1])
    high_gate(s, g[2])
    upper_gate(s, g[3], keeper(s))
    sent = [(4, q2.at[0]), (5, q2.at[1]), (6, own3), (7, give.at[1])]
    for n, (mask, _) in enumerate(sent):
        at = rows_of(reversed3(low3 ^ mask), 64)
        for c in range(2):
            part[c, pl.ds(64 * n, 64), :] = s[c, at, :]
    for mask, out in ((0, own0), (1, give.at[0]), (2, q1.at[0]), (3, q1.at[1])):
        at = rows_of(reversed3(low3 ^ mask), 64)
        for c in range(2):
            out[c] = s[c, at, :]
    lower_gates(part, g)
    for n, (_, out) in enumerate(sent):
        for c in range(2):
            out[c] = part[c, pl.ds(64 * n, 64), :]


def near_kernel(indices, own0, other0, r1, gates, keep, send, s, mh, ml):
    g = Ready(gates, (mh, ml), indices)
    for n, block in enumerate((own0, other0, r1.at[0], r1.at[1])):
        for c in range(2):
            s[c, pl.ds(64 * n, 64), :] = block[c]
    lower_gates(s, g)
    for n, out in enumerate((keep.at[0], keep.at[1], keep.at[2], send)):
        for c in range(2):
            out[c] = s[c, pl.ds(64 * n, 64), :]


def second_kernel(indices, me_ref, near, r2, r3, post1, post2, gates, own, give, y1, self0, s, mh, ml):
    g = Ready(gates, (mh, ml), indices)
    me = me_ref[0]
    low3, core = me & 7, me & 1
    blocks = (near.at[0], near.at[1], near.at[2], post1, r2.at[0], post2, r3.at[0], r3.at[1])
    for mask, block in enumerate(blocks):
        at = rows_of(reversed3(low3 ^ mask), 64)
        for c in range(2):
            s[c, at, :] = block[c]
    high_gate(s, g[6])
    upper_gate(s, g[7], keeper(s))

    def write(out, mask):
        at = rows_of(me ^ mask, 32)
        for c in range(2):
            out[c] = s[c, at, :]

    for i, base in enumerate(PORTS):
        for f in range(2):
            write(own.at[i, f], 2 * (base + core) + f)
            write(give.at[2 * i + f], 2 * (base + 1 - core) + (1 - f))
    write(give.at[6], 3)
    write(give.at[7], 1)
    write(y1, 2)
    write(self0, 0)


def gate_nine(s, g, blocks, outs):
    for n, block in enumerate(blocks):
        for c in range(2):
            s[c, pl.ds(32 * n, 32), :] = block[c]
    middle_gate(s, g[9])
    for n, out in enumerate(outs):
        for c in range(2):
            out[c] = s[c, pl.ds(32 * n, 32), :]


def before_kernel(indices, own, recv, gates, out, s, mh, ml):
    g = Ready(gates, (mh, ml), indices)
    gate_nine(s, g, (*split(own), *split(recv)), [out.at[f, src] for src in range(2) for f in range(2)])


def after_kernel(indices, a0, a1, y1, self0, other, gates, keep, send, s, mh, ml):
    g = Ready(gates, (mh, ml), indices)
    blocks = [a.at[f, src] for f in range(2) for a in (a0, a1) for src in range(2)]
    blocks = blocks[:4] + [y1.at[0], y1.at[1], self0, other] + blocks[4:]
    gate_nine(s, g, blocks, [keep.at[n] for n in range(8)] + [send.at[n] for n in range(4)])


def third_kernel(indices, me_ref, keep, early, a2, late, gates, out, s, mh, ml, y, ysems):
    g = Ready(gates, (mh, ml), indices)
    me = me_ref[0]
    core = me & 1

    def place(block, mask):
        at = rows_of(me ^ mask, 32)
        for c in range(2):
            s[c, at, :] = block[c]

    for i, base in enumerate(PORTS):
        for src in range(2):
            place(keep.at[2 * i + src] if i < 2 else a2.at[0, src], 2 * (base + core) + src)
            place(early.at[2 * i + src] if i < 2 else late.at[src], 2 * (base + 1 - core) + (1 - src))
    for n, mask in ((4, 2), (5, 3), (6, 0), (7, 1)):
        place(keep.at[n], mask)
    high_gate(s, g[10])
    copies = []

    def store(c, row, value):
        y[pl.ds(2 * row + c, LANES, stride=2), :] = value
        if c == 1 and row % PAIR == LANES:
            at = pl.ds(2 * (row - LANES), 2 * PAIR)
            copies.append(pltpu.make_async_copy(y.at[at], out.at[at], ysems.at[len(copies)]))
            copies[-1].start()

    upper_gate(s, g[11], store)
    for copy in copies:
        copy.wait()


def shape(*dims):
    return jax.ShapeDtypeStruct(dims, F32)


def call(kernel, indices, outs, rows, operands, specs, scratch=(), out_specs=None, limit=32 << 20):
    n = len(indices)
    fetch = [pltpu.VMEM((n, 2, LANES, LANES), F32), pltpu.SemaphoreType.DMA((n,))] if specs[-1] is HBM else []
    return pl.pallas_call(
        functools.partial(kernel, indices),
        out_shape=outs,
        in_specs=specs,
        out_specs=out_specs or [VMEM] * len(outs),
        scratch_shapes=[
            pltpu.VMEM((2, rows, LANES), F32),
            *fetch,
            pltpu.VMEM((n, PAIR, PAIR), BF16),
            pltpu.VMEM((n, PAIR, PAIR), BF16),
            *scratch,
        ],
        compiler_params=pltpu.CompilerParams(vmem_limit_bytes=limit),
        name=kernel.__name__,
    )(*operands)


def flipped(block, mask, port=0):
    route = [(i, i ^ mask ^ (port if i & 1 else 0)) for i in range(lax.axis_size("node"))]
    return lax.ppermute(block, "node", route)


def fast_body(amplitudes, gates):
    total = amplitudes.shape[1]
    rows = total // LANES
    eighth, part16 = rows // 8, rows // 16
    me = lax.axis_index("node").astype(jnp.int32).reshape(1)
    x = amplitudes.reshape(2, rows, LANES).transpose(1, 0, 2).reshape(2 * rows, LANES)
    interleaved = (pltpu.VMEM((2 * rows, LANES), F32), pltpu.SemaphoreType.DMA((2,)))
    one, two = shape(2, eighth, LANES), shape(2, 2, eighth, LANES)
    q1, q2, own3, own0, give = call(
        first_kernel,
        (0, 1, 2, 3, 4, 5, 8),
        [two, two, one, one, two],
        rows,
        [me, x, gates],
        [SMEM, HBM, HBM],
        (*interleaved, pltpu.VMEM((2, 4 * eighth, LANES), F32)),
        limit=532 * 104858,
    )
    recv = flipped(give, 1)
    r1, r2 = flipped(q1, 2), flipped(q2, 4)
    r3 = flipped(jnp.stack([own3, recv[1]]), 6)
    near, send = call(
        near_kernel,
        (4, 5, 8),
        [shape(3, 2, eighth, LANES), one],
        4 * eighth,
        [own0, recv[0], r1, gates],
        [VMEM] * 4,
    )
    post1, post2 = flipped(send, 1), flipped(r2[1], 1)
    block = (2, part16, LANES)
    own, give, y1, self0 = call(
        second_kernel,
        (6, 7),
        [shape(3, 2, *block), shape(8, *block), shape(*block), shape(*block)],
        rows,
        [me, near, r2, r3, post1, post2, gates],
        [SMEM] + [VMEM] * 6,
    )
    recv = flipped(give, 1)
    ready = call(
        before_kernel, (9,), [shape(2, 2, *block)], 4 * part16, [own[2], recv[4:6], gates], [VMEM] * 3
    )[0]
    payloads = [jnp.stack([own[i], recv[2 * i : 2 * i + 2]], 1) for i in range(2)] + [ready]
    a0, a1, a2 = [flipped(payload, 2 * base, 2) for base, payload in zip(PORTS, payloads)]
    y1 = flipped(jnp.stack([y1, recv[6]]), 2)
    keep, send = call(
        after_kernel,
        (9,),
        [shape(8, *block), shape(4, *block)],
        12 * part16,
        [a0, a1, y1, self0, recv[7], gates],
        [VMEM] * 6,
    )
    early, late = flipped(send, 1), flipped(a2[1], 1)
    out = call(
        third_kernel,
        (10, 11),
        [shape(2 * rows, LANES)],
        rows,
        [me, keep, early, a2, late, gates],
        [SMEM] + [VMEM] * 5,
        interleaved,
        [HBM],
    )[0]
    return out.reshape(rows, 2, LANES).transpose(1, 0, 2).reshape(2, total)


def swapped(block, axis, apart):
    count = lax.axis_size(axis)
    route = []
    for low in range(count):
        high = low | 1 << apart
        if high != low and high < count:
            route += [(low, high), (high, low)]
    return lax.ppermute(block, axis, route)


def apply_gate(state, gate_pair, offset):
    total = state.shape[1]
    real_g, imag_g = (gate_pair[0], gate_pair[1])
    hp = lax.Precision.HIGHEST
    if offset == 0:
        view = state.reshape(2, total // 128, 128)
        real_in, imag_in = (view[0], view[1])
        real_out = jnp.einsum("ij,aj->ai", real_g, real_in, precision=hp) - jnp.einsum(
            "ij,aj->ai", imag_g, imag_in, precision=hp
        )
        imag_out = jnp.einsum("ij,aj->ai", real_g, imag_in, precision=hp) + jnp.einsum(
            "ij,aj->ai", imag_g, real_in, precision=hp
        )
        return jnp.stack([real_out, imag_out], 0).reshape(2, total)
    inner = 1 << offset
    outer = total // (128 * inner)
    folded = 1
    if inner < 128:
        folded = min(128 // inner, outer)
    view = state.reshape(2, outer // folded, folded, 128, inner)
    view = jnp.transpose(view, (0, 1, 3, 2, 4)).reshape(2, outer // folded, 128, folded * inner)
    real_in, imag_in = (view[0], view[1])
    real_out = jnp.einsum("ij,ajb->aib", real_g, real_in, precision=hp) - jnp.einsum(
        "ij,ajb->aib", imag_g, imag_in, precision=hp
    )
    imag_out = jnp.einsum("ij,ajb->aib", real_g, imag_in, precision=hp) + jnp.einsum(
        "ij,ajb->aib", imag_g, real_in, precision=hp
    )
    result = jnp.stack([real_out, imag_out], 0).reshape(2, outer // folded, 128, folded, inner)
    return jnp.transpose(result, (0, 1, 3, 2, 4)).reshape(2, total)


def run_gates(state, gates, indices, offsets):
    distinct = gates.shape[1]
    for index, offset in zip(indices, offsets):
        state = apply_gate(state, gates[:, index % distinct], offset)
    return state


def leave_alone(half):
    return half


def split_halves(state, position, bit):
    total = state.shape[1]
    mine = lax.axis_index("node") // (1 << bit) % 2
    view = state.reshape(2, total >> position + 1, 2, 1 << position)
    keep = lax.dynamic_index_in_dim(view, mine, 2, keepdims=False)
    other = lax.dynamic_index_in_dim(view, 1 - mine, 2, keepdims=False)
    return (mine, keep, other)


def join_halves(mine, keep, arrived, total):
    lower = jnp.where(mine == 0, keep, arrived)
    upper = jnp.where(mine == 0, arrived, keep)
    return jnp.stack([lower, upper], 2).reshape(2, total)


def enter_bit(state, position, bit, prepare):
    total = state.shape[1]
    mine, keep, other = split_halves(state, position, bit)
    other = prepare(other.reshape(2, total // 2)).reshape(keep.shape)
    arrived = swapped(other, "node", bit)
    keep = prepare(keep.reshape(2, total // 2)).reshape(arrived.shape)
    return join_halves(mine, keep, arrived, total)


def general_body(amplitudes, gates):
    total = amplitudes.shape[1]
    locq = total.bit_length() - 1
    devices_node = lax.axis_size("node")
    offsets = [0, (locq - 7) // 2, locq - 7, locq - 9]
    state = run_gates(amplitudes, gates, [0, 1, 2, 3], offsets)

    def early_gates(half):
        return run_gates(half, gates, [4, 5], offsets[:2])

    state = enter_bit(state, locq - 1, 0, early_gates)
    for bit in range(1, 3):
        state = enter_bit(state, locq - 1 - bit, bit, leave_alone)
    state = run_gates(state, gates, [6, 7], offsets[2:])
    blocks = state.reshape(2, devices_node, total // devices_node)
    blocks = lax.all_to_all(blocks, "node", split_axis=1, concat_axis=1, tiled=True)
    state = blocks.reshape(2, total)
    return run_gates(state, gates, [8, 9, 10, 11], offsets)


def body(amplitudes, gates):
    if amplitudes.shape[1] == 65536 and lax.axis_size("node") == 16 and gates.shape[1] == 12:
        return fast_body(amplitudes, gates)
    return general_body(amplitudes, gates)


def solution(mesh):
    in_specs = (P(None, ("paths", "node")), P())
    out_specs = P(None, ("paths", "node"))
    return jax.shard_map(body, mesh=mesh, in_specs=in_specs, out_specs=out_specs, check_vma=False)
```

```python
import functools

import jax
import jax.numpy as jnp
from jax import lax
from jax.experimental import pallas as pl
from jax.experimental.pallas import tpu as pltpu
from jax.sharding import PartitionSpec as P

F32, BF16 = jnp.float32, jnp.bfloat16
LANES = 128
PAIR = 2 * LANES
NT = (((1,), (1,)), ((), ()))
NN = (((1,), (0,)), ((), ()))
PORTS = (4, 2, 6)
SMEM = pl.BlockSpec(memory_space=pltpu.SMEM)
VMEM = pl.BlockSpec(memory_space=pltpu.VMEM)
ANY = pl.BlockSpec(memory_space=pl.ANY)
HBM = pl.BlockSpec(memory_space=pltpu.HBM)


def halves(x):
    high = x.astype(BF16)
    return high, (x - high.astype(F32)).astype(BF16)


def product(a, b, dims):
    (ah, al), (bh, bl) = a, b
    dot = functools.partial(lax.dot_general, dimension_numbers=dims, preferred_element_type=F32)
    return dot(ah, bh) + (dot(al, bh) + dot(ah, bl))


def natural_gate(g):
    return g[0], g[1]


def regrouped_gate(g):
    order = lax.broadcasted_iota(jnp.int32, (LANES, LANES), 1)
    order = (order % 16) * 8 + order // 16
    out = []
    for c in range(2):
        rows = jnp.concatenate([g[c, pl.ds(m, 16, stride=8), :] for m in range(8)], 0)
        out.append(jnp.take_along_axis(rows, order, axis=1))
    return out


def prepare(g, regroup, mh, ml):
    re, im = regrouped_gate(g) if regroup else natural_gate(g)
    for r, row in enumerate(((re, -im), (im, re))):
        for c, part in enumerate(row):
            high, low = halves(part)
            at = (pl.ds(r * LANES, LANES), pl.ds(c * LANES, LANES))
            mh[at] = high
            ml[at] = low


def right_gate(x_re, x_im, m):
    out = product(halves(jnp.concatenate([x_re, x_im], 1)), m, NT)
    return out[:, :LANES], out[:, LANES:]


def left_gate(x_re, x_im, m):
    out = product(m, halves(jnp.concatenate([x_re, x_im], 0)), NN)
    return out[:LANES], out[LANES:]


def exchange(blocks):
    blocks = list(blocks)
    lane = lax.broadcasted_iota(jnp.int32, blocks[0].shape, 1)
    for bit, shift in ((4, 64), (2, 32), (1, 16)):
        low = (lane & shift) == 0
        for k in range(8):
            if k & bit == 0:
                a, b = blocks[k], blocks[k | bit]
                t = jnp.where(low, b, a)
                t = pltpu.roll(t, 64, 1) if shift == 64 else jnp.take_along_axis(t, lane ^ shift, axis=1)
                blocks[k] = jnp.where(low, a, t)
                blocks[k | bit] = jnp.where(low, t, b)
    return blocks


def high_gate(s, m):
    for pair in range(2):
        bs = (2 * pair, 2 * pair + 1)
        x = [jnp.concatenate([s[c, pl.ds(b, LANES, stride=4), :] for b in bs], 1) for c in range(2)]
        y = left_gate(*x, m)
        for c in range(2):
            for k, b in enumerate(bs):
                s[c, pl.ds(b, LANES, stride=4), :] = y[c][:, k * LANES : (k + 1) * LANES]


def upper_gate(s, m, store):
    for pair in range(2):
        bs = (2 * pair, 2 * pair + 1)
        x = [jnp.concatenate([s[c, pl.ds(b * LANES, LANES), :] for b in bs], 1) for c in range(2)]
        y = left_gate(*x, m)
        for c in range(2):
            for k, b in enumerate(bs):
                store(c, b * LANES, y[c][:, k * LANES : (k + 1) * LANES])


def middle_gate(s, m):
    count = s.shape[1] // LANES
    for first in range(0, count, 2):
        bs = tuple(range(first, min(first + 2, count)))
        x = [
            jnp.concatenate(
                [
                    jnp.concatenate(exchange([s[c, pl.ds(b * LANES + 16 * k, 16), :] for k in range(8)]), 0)
                    for b in bs
                ],
                1,
            )
            for c in range(2)
        ]
        y = left_gate(*x, m)
        for c in range(2):
            for n, b in enumerate(bs):
                part = y[c][:, n * LANES : (n + 1) * LANES]
                back = exchange([part[16 * k : 16 * k + 16] for k in range(8)])
                s[c, pl.ds(b * LANES, LANES), :] = jnp.concatenate(back, 0)


def low_gate(s, m):
    count = s.shape[1]
    for first in range(0, count, PAIR):
        at = pl.ds(first, min(PAIR, count - first))
        y = right_gate(s[0, at, :], s[1, at, :], m)
        for c in range(2):
            s[c, at, :] = y[c]


def keeper(s):
    def store(c, row, value):
        s[c, pl.ds(row, LANES), :] = value

    return store


def reversed3(v):
    return ((v & 1) << 2) | (v & 2) | ((v >> 2) & 1)


def rows_of(block, size):
    return pl.ds(pl.multiple_of(block * size, size), size)


def split(ref):
    return ref.at[0], ref.at[1]


class Gates:
    def __init__(self, source, scratch, indices):
        self.own, self.sems, self.mh, self.ml = scratch
        self.indices = indices
        self.copies = [
            pltpu.make_async_copy(source.at[:, g], self.own.at[k], self.sems.at[k]) for k, g in enumerate(indices)
        ]

    def start(self, ks):
        for k in ks:
            self.copies[k].start()

    def ready(self, ks):
        for k in ks:
            self.copies[k].wait()
        for k in ks:
            prepare(self.own.at[k], self.indices[k] % 4 == 1, self.mh.at[k], self.ml.at[k])

    def __getitem__(self, g):
        k = self.indices.index(g)
        return self.mh[k], self.ml[k]


class Ready:
    def __init__(self, source, scratch, indices):
        self.mh, self.ml = scratch
        self.indices = indices
        for k, g in enumerate(indices):
            prepare(source.at[:, g], g % 4 == 1, self.mh.at[k], self.ml.at[k])

    def __getitem__(self, g):
        k = self.indices.index(g)
        return self.mh[k], self.ml[k]


def first_kernel(indices, me_ref, amps, gates, q2, q1, own3, own0, give, s, own, sems, mh, ml, x, xsems):
    g = Gates(gates, (own, sems, mh, ml), indices)
    parts = []
    for b in range(2):
        at = pl.ds(2 * PAIR * b, 2 * PAIR)
        parts.append(pltpu.make_async_copy(amps.at[at], x.at[at], xsems.at[b]))
    g.start([0])
    for copy in parts:
        copy.start()
    g.start(range(1, len(indices)))
    low3 = me_ref[0] & 7
    g.ready([0])
    for b in range(2):
        parts[b].wait()
        y = right_gate(*[x[pl.ds(2 * PAIR * b + c, PAIR, stride=2), :] for c in range(2)], g[0])
        for c in range(2):
            s[c, pl.ds(b * PAIR, PAIR), :] = y[c]
    g.ready(range(1, len(indices)))
    middle_gate(s, g[1])
    high_gate(s, g[2])
    upper_gate(s, g[3], keeper(s))
    for mask, out in enumerate((own0, give.at[0], *split(q1), *split(q2), own3, give.at[1])):
        at = rows_of(reversed3(low3 ^ mask), 64)
        for c in range(2):
            out[c] = s[c, at, :]


def lower_blocks(s, g, blocks, outs):
    for n, block in enumerate(blocks):
        for c in range(2):
            s[c, pl.ds(64 * n, 64), :] = block[c]
    low_gate(s, g[4])
    middle_gate(s, g[5])
    low_gate(s, g[8])
    for n, out in enumerate(outs):
        for c in range(2):
            out[c] = s[c, pl.ds(64 * n, 64), :]


def before_lower(indices, own0, own3, recv, gates, p0, p3, s, mh, ml):
    g = Ready(gates, (mh, ml), indices)
    lower_blocks(s, g, (own0, recv.at[0], own3, recv.at[1]), (*split(p0), *split(p3)))


def after_lower(indices, r1, r2, gates, keep, send1, send2, s, mh, ml):
    g = Ready(gates, (mh, ml), indices)
    lower_blocks(s, g, (*split(r1), *split(r2)), (keep.at[0], send1, keep.at[1], send2))


def second_kernel(indices, me_ref, p0, near, r3, post1, post2, gates, own, give, y1, self0, s, mh, ml):
    g = Ready(gates, (mh, ml), indices)
    me = me_ref[0]
    low3, core = me & 7, me & 1
    blocks = (*split(p0), near.at[0], post1, near.at[1], post2, *split(r3))
    for mask, block in enumerate(blocks):
        at = rows_of(reversed3(low3 ^ mask), 64)
        for c in range(2):
            s[c, at, :] = block[c]
    high_gate(s, g[6])
    upper_gate(s, g[7], keeper(s))

    def write(out, mask):
        at = rows_of(me ^ mask, 32)
        for c in range(2):
            out[c] = s[c, at, :]

    for i, base in enumerate(PORTS):
        for f in range(2):
            write(own.at[i, f], 2 * (base + core) + f)
            write(give.at[2 * i + f], 2 * (base + 1 - core) + (1 - f))
    write(give.at[6], 3)
    write(give.at[7], 1)
    write(y1, 2)
    write(self0, 0)


def gate_nine(s, g, blocks, outs):
    for n, block in enumerate(blocks):
        for c in range(2):
            s[c, pl.ds(32 * n, 32), :] = block[c]
    middle_gate(s, g[9])
    for n, out in enumerate(outs):
        for c in range(2):
            out[c] = s[c, pl.ds(32 * n, 32), :]


def before_kernel(indices, own, recv, gates, out, s, mh, ml):
    g = Ready(gates, (mh, ml), indices)
    gate_nine(s, g, (*split(own), *split(recv)), [out.at[f, src] for src in range(2) for f in range(2)])


def after_kernel(indices, a0, a1, y1, self0, other, gates, keep, send, s, mh, ml):
    g = Ready(gates, (mh, ml), indices)
    blocks = [a.at[f, src] for f in range(2) for a in (a0, a1) for src in range(2)]
    blocks = blocks[:4] + [y1.at[0], y1.at[1], self0, other] + blocks[4:]
    gate_nine(s, g, blocks, [keep.at[n] for n in range(8)] + [send.at[n] for n in range(4)])


def third_kernel(indices, me_ref, keep, early, a2, late, gates, out, s, mh, ml, y, ysems):
    g = Ready(gates, (mh, ml), indices)
    me = me_ref[0]
    core = me & 1

    def place(block, mask):
        at = rows_of(me ^ mask, 32)
        for c in range(2):
            s[c, at, :] = block[c]

    for i, base in enumerate(PORTS):
        for src in range(2):
            place(keep.at[2 * i + src] if i < 2 else a2.at[0, src], 2 * (base + core) + src)
            place(early.at[2 * i + src] if i < 2 else late.at[src], 2 * (base + 1 - core) + (1 - src))
    for n, mask in ((4, 2), (5, 3), (6, 0), (7, 1)):
        place(keep.at[n], mask)
    high_gate(s, g[10])
    copies = []

    def store(c, row, value):
        y[pl.ds(2 * row + c, LANES, stride=2), :] = value
        if c == 1 and row % PAIR == LANES:
            at = pl.ds(2 * (row - LANES), 2 * PAIR)
            copies.append(pltpu.make_async_copy(y.at[at], out.at[at], ysems.at[len(copies)]))
            copies[-1].start()

    upper_gate(s, g[11], store)
    for copy in copies:
        copy.wait()


def shape(*dims):
    return jax.ShapeDtypeStruct(dims, F32)


COST = {name: pl.CostEstimate(flops=n, bytes_accessed=1 << 18, transcendentals=0) for name, n in {"after_kernel": 2000000000, "after_lower": 2000000000, "before_kernel": 1000000000, "before_lower": 2000000000}.items()}


def call(kernel, indices, outs, rows, operands, specs, scratch=(), out_specs=None, limit=32 << 20):
    n = len(indices)
    fetch = [pltpu.VMEM((n, 2, LANES, LANES), F32), pltpu.SemaphoreType.DMA((n,))] if specs[-1] is HBM else []
    return pl.pallas_call(
        functools.partial(kernel, indices),
        out_shape=outs,
        in_specs=specs,
        out_specs=out_specs or [VMEM] * len(outs),
        scratch_shapes=[
            pltpu.VMEM((2, rows, LANES), F32),
            *fetch,
            pltpu.VMEM((n, PAIR, PAIR), BF16),
            pltpu.VMEM((n, PAIR, PAIR), BF16),
            *scratch,
        ],
        compiler_params=pltpu.CompilerParams(vmem_limit_bytes=limit),
        name=kernel.__name__,
        cost_estimate=COST.get(kernel.__name__),
    )(*operands)


def flipped(block, mask, port=0):
    route = [(i, i ^ mask ^ (port if i & 1 else 0)) for i in range(lax.axis_size("node"))]
    return lax.ppermute(block, "node", route)


def fast_body(amplitudes, gates):
    total = amplitudes.shape[1]
    rows = total // LANES
    eighth, part16 = rows // 8, rows // 16
    me = lax.axis_index("node").astype(jnp.int32).reshape(1)
    x = amplitudes.reshape(2, rows, LANES).transpose(1, 0, 2).reshape(2 * rows, LANES)
    interleaved = (pltpu.VMEM((2 * rows, LANES), F32), pltpu.SemaphoreType.DMA((2,)))
    one, two = shape(2, eighth, LANES), shape(2, 2, eighth, LANES)
    q2, q1, own3, own0, give = call(
        first_kernel,
        (0, 1, 2, 3),
        [two, two, one, one, two],
        rows,
        [me, x, gates],
        [SMEM, HBM, HBM],
        interleaved,
        limit=532 * 104858,
    )
    recv = flipped(give, 1)
    r1, r2 = flipped(q1, 2), flipped(q2, 4)
    p0, p3 = call(before_lower, (4, 5, 8), [two, two], 4 * eighth, [own0, own3, recv, gates], [VMEM] * 4)
    r3 = flipped(p3, 6)
    near, send1, send2 = call(after_lower, (4, 5, 8), [two, one, one], 4 * eighth, [r1, r2, gates], [VMEM] * 3)
    post1, post2 = flipped(send1, 1), flipped(send2, 1)
    block = (2, part16, LANES)
    own, give, y1, self0 = call(
        second_kernel,
        (6, 7),
        [shape(3, 2, *block), shape(8, *block), shape(*block), shape(*block)],
        rows,
        [me, p0, near, r3, post1, post2, gates],
        [SMEM] + [VMEM] * 6,
    )
    recv = flipped(give, 1)
    ready = call(
        before_kernel, (9,), [shape(2, 2, *block)], 4 * part16, [own[2], recv[4:6], gates], [VMEM] * 3
    )[0]
    payloads = [jnp.stack([own[i], recv[2 * i : 2 * i + 2]], 1) for i in range(2)] + [ready]
    a0, a1, a2 = [flipped(payload, 2 * base, 2) for base, payload in zip(PORTS, payloads)]
    y1 = flipped(jnp.stack([y1, recv[6]]), 2)
    keep, send = call(
        after_kernel,
        (9,),
        [shape(8, *block), shape(4, *block)],
        12 * part16,
        [a0, a1, y1, self0, recv[7], gates],
        [VMEM] * 6,
    )
    early, late = flipped(send, 1), flipped(a2[1], 1)
    out = call(
        third_kernel,
        (10, 11),
        [shape(2 * rows, LANES)],
        rows,
        [me, keep, early, a2, late, gates],
        [SMEM] + [VMEM] * 5,
        interleaved,
        [HBM],
    )[0]
    return out.reshape(rows, 2, LANES).transpose(1, 0, 2).reshape(2, total)


def swapped(block, axis, apart):
    count = lax.axis_size(axis)
    route = []
    for low in range(count):
        high = low | 1 << apart
        if high != low and high < count:
            route += [(low, high), (high, low)]
    return lax.ppermute(block, axis, route)


def apply_gate(state, gate_pair, offset):
    total = state.shape[1]
    real_g, imag_g = (gate_pair[0], gate_pair[1])
    hp = lax.Precision.HIGHEST
    if offset == 0:
        view = state.reshape(2, total // 128, 128)
        real_in, imag_in = (view[0], view[1])
        real_out = jnp.einsum("ij,aj->ai", real_g, real_in, precision=hp) - jnp.einsum(
            "ij,aj->ai", imag_g, imag_in, precision=hp
        )
        imag_out = jnp.einsum("ij,aj->ai", real_g, imag_in, precision=hp) + jnp.einsum(
            "ij,aj->ai", imag_g, real_in, precision=hp
        )
        return jnp.stack([real_out, imag_out], 0).reshape(2, total)
    inner = 1 << offset
    outer = total // (128 * inner)
    folded = 1
    if inner < 128:
        folded = min(128 // inner, outer)
    view = state.reshape(2, outer // folded, folded, 128, inner)
    view = jnp.transpose(view, (0, 1, 3, 2, 4)).reshape(2, outer // folded, 128, folded * inner)
    real_in, imag_in = (view[0], view[1])
    real_out = jnp.einsum("ij,ajb->aib", real_g, real_in, precision=hp) - jnp.einsum(
        "ij,ajb->aib", imag_g, imag_in, precision=hp
    )
    imag_out = jnp.einsum("ij,ajb->aib", real_g, imag_in, precision=hp) + jnp.einsum(
        "ij,ajb->aib", imag_g, real_in, precision=hp
    )
    result = jnp.stack([real_out, imag_out], 0).reshape(2, outer // folded, 128, folded, inner)
    return jnp.transpose(result, (0, 1, 3, 2, 4)).reshape(2, total)


def run_gates(state, gates, indices, offsets):
    distinct = gates.shape[1]
    for index, offset in zip(indices, offsets):
        state = apply_gate(state, gates[:, index % distinct], offset)
    return state


def leave_alone(half):
    return half


def split_halves(state, position, bit):
    total = state.shape[1]
    mine = lax.axis_index("node") // (1 << bit) % 2
    view = state.reshape(2, total >> position + 1, 2, 1 << position)
    keep = lax.dynamic_index_in_dim(view, mine, 2, keepdims=False)
    other = lax.dynamic_index_in_dim(view, 1 - mine, 2, keepdims=False)
    return (mine, keep, other)


def join_halves(mine, keep, arrived, total):
    lower = jnp.where(mine == 0, keep, arrived)
    upper = jnp.where(mine == 0, arrived, keep)
    return jnp.stack([lower, upper], 2).reshape(2, total)


def enter_bit(state, position, bit, prepare):
    total = state.shape[1]
    mine, keep, other = split_halves(state, position, bit)
    other = prepare(other.reshape(2, total // 2)).reshape(keep.shape)
    arrived = swapped(other, "node", bit)
    keep = prepare(keep.reshape(2, total // 2)).reshape(arrived.shape)
    return join_halves(mine, keep, arrived, total)


def general_body(amplitudes, gates):
    total = amplitudes.shape[1]
    locq = total.bit_length() - 1
    devices_node = lax.axis_size("node")
    offsets = [0, (locq - 7) // 2, locq - 7, locq - 9]
    state = run_gates(amplitudes, gates, [0, 1, 2, 3], offsets)

    def early_gates(half):
        return run_gates(half, gates, [4, 5], offsets[:2])

    state = enter_bit(state, locq - 1, 0, early_gates)
    for bit in range(1, 3):
        state = enter_bit(state, locq - 1 - bit, bit, leave_alone)
    state = run_gates(state, gates, [6, 7], offsets[2:])
    blocks = state.reshape(2, devices_node, total // devices_node)
    blocks = lax.all_to_all(blocks, "node", split_axis=1, concat_axis=1, tiled=True)
    state = blocks.reshape(2, total)
    return run_gates(state, gates, [8, 9, 10, 11], offsets)


def body(amplitudes, gates):
    if amplitudes.shape[1] == 65536 and lax.axis_size("node") == 16 and gates.shape[1] == 12:
        return fast_body(amplitudes, gates)
    return general_body(amplitudes, gates)


def solution(mesh):
    in_specs = (P(None, ("paths", "node")), P())
    out_specs = P(None, ("paths", "node"))
    return jax.shard_map(body, mesh=mesh, in_specs=in_specs, out_specs=out_specs, check_vma=False)
```

```python
import functools

import jax
import jax.numpy as jnp
from jax import lax
from jax.experimental import pallas as pl
from jax.experimental.pallas import tpu as pltpu
from jax.sharding import PartitionSpec as P

F32, BF16 = jnp.float32, jnp.bfloat16
LANES = 128
PAIR = 2 * LANES
NT = (((1,), (1,)), ((), ()))
NN = (((1,), (0,)), ((), ()))
PORTS = (4, 2, 6)
SMEM = pl.BlockSpec(memory_space=pltpu.SMEM)
VMEM = pl.BlockSpec(memory_space=pltpu.VMEM)
ANY = pl.BlockSpec(memory_space=pl.ANY)
HBM = pl.BlockSpec(memory_space=pltpu.HBM)


def halves(x):
    high = x.astype(BF16)
    return high, (x - high.astype(F32)).astype(BF16)


def product(a, b, dims):
    (ah, al), (bh, bl) = a, b
    dot = functools.partial(lax.dot_general, dimension_numbers=dims, preferred_element_type=F32)
    return dot(ah, bh) + (dot(al, bh) + dot(ah, bl))


def natural_gate(g):
    return g[0], g[1]


def regrouped_gate(g):
    order = lax.broadcasted_iota(jnp.int32, (LANES, LANES), 1)
    order = (order % 16) * 8 + order // 16
    out = []
    for c in range(2):
        rows = jnp.concatenate([g[c, pl.ds(m, 16, stride=8), :] for m in range(8)], 0)
        out.append(jnp.take_along_axis(rows, order, axis=1))
    return out


def prepare(g, regroup, mh, ml):
    re, im = regrouped_gate(g) if regroup else natural_gate(g)
    for r, row in enumerate(((re, -im), (im, re))):
        for c, part in enumerate(row):
            high, low = halves(part)
            at = (pl.ds(r * LANES, LANES), pl.ds(c * LANES, LANES))
            mh[at] = high
            ml[at] = low


def right_gate(x_re, x_im, m):
    out = product(halves(jnp.concatenate([x_re, x_im], 1)), m, NT)
    return out[:, :LANES], out[:, LANES:]


def left_gate(x_re, x_im, m):
    out = product(m, halves(jnp.concatenate([x_re, x_im], 0)), NN)
    return out[:LANES], out[LANES:]


def exchange(blocks):
    blocks = list(blocks)
    lane = lax.broadcasted_iota(jnp.int32, blocks[0].shape, 1)
    for bit, shift in ((4, 64), (2, 32), (1, 16)):
        low = (lane & shift) == 0
        for k in range(8):
            if k & bit == 0:
                a, b = blocks[k], blocks[k | bit]
                t = jnp.where(low, b, a)
                t = pltpu.roll(t, 64, 1) if shift == 64 else jnp.take_along_axis(t, lane ^ shift, axis=1)
                blocks[k] = jnp.where(low, a, t)
                blocks[k | bit] = jnp.where(low, t, b)
    return blocks


def high_gate(s, m):
    for pair in range(2):
        bs = (2 * pair, 2 * pair + 1)
        x = [jnp.concatenate([s[c, pl.ds(b, LANES, stride=4), :] for b in bs], 1) for c in range(2)]
        y = left_gate(*x, m)
        for c in range(2):
            for k, b in enumerate(bs):
                s[c, pl.ds(b, LANES, stride=4), :] = y[c][:, k * LANES : (k + 1) * LANES]


def upper_gate(s, m, store):
    for pair in range(2):
        bs = (2 * pair, 2 * pair + 1)
        x = [jnp.concatenate([s[c, pl.ds(b * LANES, LANES), :] for b in bs], 1) for c in range(2)]
        y = left_gate(*x, m)
        for c in range(2):
            for k, b in enumerate(bs):
                store(c, b * LANES, y[c][:, k * LANES : (k + 1) * LANES])


def middle_gate(s, m):
    count = s.shape[1] // LANES
    for first in range(0, count, 2):
        bs = tuple(range(first, min(first + 2, count)))
        x = [
            jnp.concatenate(
                [
                    jnp.concatenate(exchange([s[c, pl.ds(b * LANES + 16 * k, 16), :] for k in range(8)]), 0)
                    for b in bs
                ],
                1,
            )
            for c in range(2)
        ]
        y = left_gate(*x, m)
        for c in range(2):
            for n, b in enumerate(bs):
                part = y[c][:, n * LANES : (n + 1) * LANES]
                back = exchange([part[16 * k : 16 * k + 16] for k in range(8)])
                s[c, pl.ds(b * LANES, LANES), :] = jnp.concatenate(back, 0)


def low_gate(s, m):
    count = s.shape[1]
    for first in range(0, count, PAIR):
        at = pl.ds(first, min(PAIR, count - first))
        y = right_gate(s[0, at, :], s[1, at, :], m)
        for c in range(2):
            s[c, at, :] = y[c]


def keeper(s):
    def store(c, row, value):
        s[c, pl.ds(row, LANES), :] = value

    return store


def reversed3(v):
    return ((v & 1) << 2) | (v & 2) | ((v >> 2) & 1)


def rows_of(block, size):
    return pl.ds(pl.multiple_of(block * size, size), size)


def split(ref):
    return ref.at[0], ref.at[1]


class Gates:
    def __init__(self, source, scratch, indices):
        self.own, self.sems, self.mh, self.ml = scratch
        self.indices = indices
        self.copies = [
            pltpu.make_async_copy(source.at[:, g], self.own.at[k], self.sems.at[k]) for k, g in enumerate(indices)
        ]

    def start(self, ks):
        for k in ks:
            self.copies[k].start()

    def ready(self, ks):
        for k in ks:
            self.copies[k].wait()
        for k in ks:
            prepare(self.own.at[k], self.indices[k] % 4 == 1, self.mh.at[k], self.ml.at[k])

    def __getitem__(self, g):
        k = self.indices.index(g)
        return self.mh[k], self.ml[k]


class Ready:
    def __init__(self, source, scratch, indices):
        self.mh, self.ml = scratch
        self.indices = indices
        for k, g in enumerate(indices):
            prepare(source.at[:, g], g % 4 == 1, self.mh.at[k], self.ml.at[k])

    def __getitem__(self, g):
        k = self.indices.index(g)
        return self.mh[k], self.ml[k]


def first_kernel(indices, me_ref, amps, gates, q2, q1, own3, own0, give, s, own, sems, mh, ml, x, xsems):
    g = Gates(gates, (own, sems, mh, ml), indices)
    parts = []
    for b in range(2):
        at = pl.ds(2 * PAIR * b, 2 * PAIR)
        parts.append(pltpu.make_async_copy(amps.at[at], x.at[at], xsems.at[b]))
    g.start([0])
    for copy in parts:
        copy.start()
    g.start(range(1, len(indices)))
    low3 = me_ref[0] & 7
    g.ready([0])
    for b in range(2):
        parts[b].wait()
        y = right_gate(*[x[pl.ds(2 * PAIR * b + c, PAIR, stride=2), :] for c in range(2)], g[0])
        for c in range(2):
            s[c, pl.ds(b * PAIR, PAIR), :] = y[c]
    g.ready(range(1, len(indices)))
    middle_gate(s, g[1])
    high_gate(s, g[2])
    upper_gate(s, g[3], keeper(s))
    for mask, out in enumerate((own0, give.at[0], *split(q1), *split(q2), own3, give.at[1])):
        at = rows_of(reversed3(low3 ^ mask), 64)
        for c in range(2):
            out[c] = s[c, at, :]


def lower_blocks(s, g, blocks, outs):
    for n, block in enumerate(blocks):
        for c in range(2):
            s[c, pl.ds(64 * n, 64), :] = block[c]
    low_gate(s, g[4])
    middle_gate(s, g[5])
    low_gate(s, g[8])
    for n, out in enumerate(outs):
        for c in range(2):
            out[c] = s[c, pl.ds(64 * n, 64), :]


def before_lower(indices, own0, own3, recv, gates, p0, p3, s, mh, ml):
    g = Ready(gates, (mh, ml), indices)
    lower_blocks(s, g, (own0, recv.at[0], own3, recv.at[1]), (*split(p0), *split(p3)))


def after_lower(indices, r1, r2, gates, keep, send1, send2, s, mh, ml):
    g = Ready(gates, (mh, ml), indices)
    lower_blocks(s, g, (*split(r1), *split(r2)), (keep.at[0], send1, keep.at[1], send2))


def second_kernel(indices, me_ref, p0, near, r3, post1, post2, gates, own, give, y1, self0, s, mh, ml):
    g = Ready(gates, (mh, ml), indices)
    me = me_ref[0]
    low3, core = me & 7, me & 1
    blocks = (*split(p0), near.at[0], post1, near.at[1], post2, *split(r3))
    for mask, block in enumerate(blocks):
        at = rows_of(reversed3(low3 ^ mask), 64)
        for c in range(2):
            s[c, at, :] = block[c]
    high_gate(s, g[6])
    upper_gate(s, g[7], keeper(s))

    def write(out, mask):
        at = rows_of(me ^ mask, 32)
        for c in range(2):
            out[c] = s[c, at, :]

    for i, base in enumerate(PORTS):
        for f in range(2):
            write(own.at[i, f], 2 * (base + core) + f)
            write(give.at[2 * i + f], 2 * (base + 1 - core) + (1 - f))
    write(give.at[6], 3)
    write(give.at[7], 1)
    write(y1, 2)
    write(self0, 0)


def gate_nine(s, g, blocks, outs):
    for n, block in enumerate(blocks):
        for c in range(2):
            s[c, pl.ds(32 * n, 32), :] = block[c]
    middle_gate(s, g[9])
    for n, out in enumerate(outs):
        for c in range(2):
            out[c] = s[c, pl.ds(32 * n, 32), :]


def before_kernel(indices, own, recv, gates, out0, out1, s, mh, ml):
    g = Ready(gates, (mh, ml), indices)
    gate_nine(s, g, (*split(own), *split(recv)), [out.at[src] for src in range(2) for out in (out0, out1)])


def after_kernel(indices, a0, a1, y1, self0, other, gates, keep, send, s, mh, ml):
    g = Ready(gates, (mh, ml), indices)
    blocks = [a.at[f, src] for f in range(2) for a in (a0, a1) for src in range(2)]
    blocks = blocks[:4] + [y1.at[0], y1.at[1], self0, other] + blocks[4:]
    gate_nine(s, g, blocks, [keep.at[n] for n in range(8)] + [send.at[n] for n in range(4)])


def join_kernel(indices, mine, late, out, s, mh, ml):
    for n, block in enumerate((*split(mine), *split(late))):
        for c in range(2):
            out[n, c] = block[c]


def third_kernel(indices, me_ref, keep, early, far, gates, out, s, mh, ml, y, ysems):
    g = Ready(gates, (mh, ml), indices)
    me = me_ref[0]
    core = me & 1

    def place(block, mask):
        at = rows_of(me ^ mask, 32)
        for c in range(2):
            s[c, at, :] = block[c]

    for i, base in enumerate(PORTS):
        for src in range(2):
            place(keep.at[2 * i + src] if i < 2 else far.at[src], 2 * (base + core) + src)
            place(early.at[2 * i + src] if i < 2 else far.at[2 + src], 2 * (base + 1 - core) + (1 - src))
    for n, mask in ((4, 2), (5, 3), (6, 0), (7, 1)):
        place(keep.at[n], mask)
    high_gate(s, g[10])
    copies = []

    def store(c, row, value):
        y[pl.ds(2 * row + c, LANES, stride=2), :] = value
        if c == 1 and row % PAIR == LANES:
            at = pl.ds(2 * (row - LANES), 2 * PAIR)
            copies.append(pltpu.make_async_copy(y.at[at], out.at[at], ysems.at[len(copies)]))
            copies[-1].start()

    upper_gate(s, g[11], store)
    for copy in copies:
        copy.wait()


def shape(*dims):
    return jax.ShapeDtypeStruct(dims, F32)


COST = {name: pl.CostEstimate(flops=n, bytes_accessed=1 << 18, transcendentals=0) for name, n in {"join_kernel": 2000000000, "after_kernel": 2000000000, "after_lower": 2000000000, "before_kernel": 1000000000, "before_lower": 2000000000}.items()}


def call(kernel, indices, outs, rows, operands, specs, scratch=(), out_specs=None, limit=32 << 20):
    n = len(indices)
    fetch = [pltpu.VMEM((n, 2, LANES, LANES), F32), pltpu.SemaphoreType.DMA((n,))] if specs[-1] is HBM else []
    return pl.pallas_call(
        functools.partial(kernel, indices),
        out_shape=outs,
        in_specs=specs,
        out_specs=out_specs or [VMEM] * len(outs),
        scratch_shapes=[
            pltpu.VMEM((2, rows, LANES), F32),
            *fetch,
            pltpu.VMEM((n, PAIR, PAIR), BF16),
            pltpu.VMEM((n, PAIR, PAIR), BF16),
            *scratch,
        ],
        compiler_params=pltpu.CompilerParams(vmem_limit_bytes=limit),
        name=kernel.__name__,
        cost_estimate=COST.get(kernel.__name__),
    )(*operands)


def flipped(block, mask, port=0):
    route = [(i, i ^ mask ^ (port if i & 1 else 0)) for i in range(lax.axis_size("node"))]
    return lax.ppermute(block, "node", route)


def fast_body(amplitudes, gates):
    total = amplitudes.shape[1]
    rows = total // LANES
    eighth, part16 = rows // 8, rows // 16
    me = lax.axis_index("node").astype(jnp.int32).reshape(1)
    x = amplitudes.reshape(2, rows, LANES).transpose(1, 0, 2).reshape(2 * rows, LANES)
    interleaved = (pltpu.VMEM((2 * rows, LANES), F32), pltpu.SemaphoreType.DMA((2,)))
    one, two = shape(2, eighth, LANES), shape(2, 2, eighth, LANES)
    q2, q1, own3, own0, give = call(
        first_kernel,
        (0, 1, 2, 3),
        [two, two, one, one, two],
        rows,
        [me, x, gates],
        [SMEM, HBM, HBM],
        interleaved,
        limit=532 * 104858,
    )
    recv = flipped(give, 1)
    r1, r2 = flipped(q1, 2), flipped(q2, 4)
    p0, p3 = call(before_lower, (4, 5, 8), [two, two], 4 * eighth, [own0, own3, recv, gates], [VMEM] * 4)
    r3 = flipped(p3, 6)
    near, send1, send2 = call(after_lower, (4, 5, 8), [two, one, one], 4 * eighth, [r1, r2, gates], [VMEM] * 3)
    post1, post2 = flipped(send1, 1), flipped(send2, 1)
    block = (2, part16, LANES)
    own, give, y1, self0 = call(
        second_kernel,
        (6, 7),
        [shape(3, 2, *block), shape(8, *block), shape(*block), shape(*block)],
        rows,
        [me, p0, near, r3, post1, post2, gates],
        [SMEM] + [VMEM] * 6,
    )
    recv = flipped(give, 1)
    ready = call(
        before_kernel, (9,), [shape(2, *block)] * 2, 4 * part16, [own[2], recv[4:6], gates], [VMEM] * 3
    )
    payloads = [jnp.stack([own[i], recv[2 * i : 2 * i + 2]], 1) for i in range(2)]
    a0, a1 = [flipped(payload, 2 * base, 2) for base, payload in zip(PORTS, payloads)]
    mine, late = [flipped(payload, 2 * PORTS[2] + f, 2) for f, payload in enumerate(ready)]
    y1 = flipped(jnp.stack([y1, recv[6]]), 2)
    keep, send = call(
        after_kernel,
        (9,),
        [shape(8, *block), shape(4, *block)],
        12 * part16,
        [a0, a1, y1, self0, recv[7], gates],
        [VMEM] * 6,
    )
    early = flipped(send, 1)
    far = call(join_kernel, (9,), [shape(4, *block)], 8, [mine, late], [VMEM] * 2)[0]
    out = call(
        third_kernel,
        (10, 11),
        [shape(2 * rows, LANES)],
        rows,
        [me, keep, early, far, gates],
        [SMEM] + [VMEM] * 4,
        interleaved,
        [HBM],
    )[0]
    return out.reshape(rows, 2, LANES).transpose(1, 0, 2).reshape(2, total)


def swapped(block, axis, apart):
    count = lax.axis_size(axis)
    route = []
    for low in range(count):
        high = low | 1 << apart
        if high != low and high < count:
            route += [(low, high), (high, low)]
    return lax.ppermute(block, axis, route)


def apply_gate(state, gate_pair, offset):
    total = state.shape[1]
    real_g, imag_g = (gate_pair[0], gate_pair[1])
    hp = lax.Precision.HIGHEST
    if offset == 0:
        view = state.reshape(2, total // 128, 128)
        real_in, imag_in = (view[0], view[1])
        real_out = jnp.einsum("ij,aj->ai", real_g, real_in, precision=hp) - jnp.einsum(
            "ij,aj->ai", imag_g, imag_in, precision=hp
        )
        imag_out = jnp.einsum("ij,aj->ai", real_g, imag_in, precision=hp) + jnp.einsum(
            "ij,aj->ai", imag_g, real_in, precision=hp
        )
        return jnp.stack([real_out, imag_out], 0).reshape(2, total)
    inner = 1 << offset
    outer = total // (128 * inner)
    folded = 1
    if inner < 128:
        folded = min(128 // inner, outer)
    view = state.reshape(2, outer // folded, folded, 128, inner)
    view = jnp.transpose(view, (0, 1, 3, 2, 4)).reshape(2, outer // folded, 128, folded * inner)
    real_in, imag_in = (view[0], view[1])
    real_out = jnp.einsum("ij,ajb->aib", real_g, real_in, precision=hp) - jnp.einsum(
        "ij,ajb->aib", imag_g, imag_in, precision=hp
    )
    imag_out = jnp.einsum("ij,ajb->aib", real_g, imag_in, precision=hp) + jnp.einsum(
        "ij,ajb->aib", imag_g, real_in, precision=hp
    )
    result = jnp.stack([real_out, imag_out], 0).reshape(2, outer // folded, 128, folded, inner)
    return jnp.transpose(result, (0, 1, 3, 2, 4)).reshape(2, total)


def run_gates(state, gates, indices, offsets):
    distinct = gates.shape[1]
    for index, offset in zip(indices, offsets):
        state = apply_gate(state, gates[:, index % distinct], offset)
    return state


def leave_alone(half):
    return half


def split_halves(state, position, bit):
    total = state.shape[1]
    mine = lax.axis_index("node") // (1 << bit) % 2
    view = state.reshape(2, total >> position + 1, 2, 1 << position)
    keep = lax.dynamic_index_in_dim(view, mine, 2, keepdims=False)
    other = lax.dynamic_index_in_dim(view, 1 - mine, 2, keepdims=False)
    return (mine, keep, other)


def join_halves(mine, keep, arrived, total):
    lower = jnp.where(mine == 0, keep, arrived)
    upper = jnp.where(mine == 0, arrived, keep)
    return jnp.stack([lower, upper], 2).reshape(2, total)


def enter_bit(state, position, bit, prepare):
    total = state.shape[1]
    mine, keep, other = split_halves(state, position, bit)
    other = prepare(other.reshape(2, total // 2)).reshape(keep.shape)
    arrived = swapped(other, "node", bit)
    keep = prepare(keep.reshape(2, total // 2)).reshape(arrived.shape)
    return join_halves(mine, keep, arrived, total)


def general_body(amplitudes, gates):
    total = amplitudes.shape[1]
    locq = total.bit_length() - 1
    devices_node = lax.axis_size("node")
    offsets = [0, (locq - 7) // 2, locq - 7, locq - 9]
    state = run_gates(amplitudes, gates, [0, 1, 2, 3], offsets)

    def early_gates(half):
        return run_gates(half, gates, [4, 5], offsets[:2])

    state = enter_bit(state, locq - 1, 0, early_gates)
    for bit in range(1, 3):
        state = enter_bit(state, locq - 1 - bit, bit, leave_alone)
    state = run_gates(state, gates, [6, 7], offsets[2:])
    blocks = state.reshape(2, devices_node, total // devices_node)
    blocks = lax.all_to_all(blocks, "node", split_axis=1, concat_axis=1, tiled=True)
    state = blocks.reshape(2, total)
    return run_gates(state, gates, [8, 9, 10, 11], offsets)


def body(amplitudes, gates):
    if amplitudes.shape[1] == 65536 and lax.axis_size("node") == 16 and gates.shape[1] == 12:
        return fast_body(amplitudes, gates)
    return general_body(amplitudes, gates)


def solution(mesh):
    in_specs = (P(None, ("paths", "node")), P())
    out_specs = P(None, ("paths", "node"))
    return jax.shard_map(body, mesh=mesh, in_specs=in_specs, out_specs=out_specs, check_vma=False)
```

```python
import functools

import jax
import jax.numpy as jnp
from jax import lax
from jax.experimental import pallas as pl
from jax.experimental.pallas import tpu as pltpu
from jax.sharding import PartitionSpec as P

F32, BF16 = jnp.float32, jnp.bfloat16
LANES = 128
PAIR = 2 * LANES
NT = (((1,), (1,)), ((), ()))
NN = (((1,), (0,)), ((), ()))
PORTS = (4, 2, 6)
SMEM = pl.BlockSpec(memory_space=pltpu.SMEM)
VMEM = pl.BlockSpec(memory_space=pltpu.VMEM)
ANY = pl.BlockSpec(memory_space=pl.ANY)
HBM = pl.BlockSpec(memory_space=pltpu.HBM)


def halves(x):
    high = x.astype(BF16)
    return high, (x - high.astype(F32)).astype(BF16)


def product(a, b, dims):
    (ah, al), (bh, bl) = a, b
    dot = functools.partial(lax.dot_general, dimension_numbers=dims, preferred_element_type=F32)
    return dot(ah, bh) + (dot(al, bh) + dot(ah, bl))


def natural_gate(g):
    return g[0], g[1]


def regrouped_gate(g):
    order = lax.broadcasted_iota(jnp.int32, (LANES, LANES), 1)
    order = (order % 16) * 8 + order // 16
    out = []
    for c in range(2):
        rows = jnp.concatenate([g[c, pl.ds(m, 16, stride=8), :] for m in range(8)], 0)
        out.append(jnp.take_along_axis(rows, order, axis=1))
    return out


def prepare(g, regroup, mh, ml):
    re, im = regrouped_gate(g) if regroup else natural_gate(g)
    for r, row in enumerate(((re, -im), (im, re))):
        for c, part in enumerate(row):
            high, low = halves(part)
            at = (pl.ds(r * LANES, LANES), pl.ds(c * LANES, LANES))
            mh[at] = high
            ml[at] = low


def right_gate(x_re, x_im, m):
    out = product(halves(jnp.concatenate([x_re, x_im], 1)), m, NT)
    return out[:, :LANES], out[:, LANES:]


def left_gate(x_re, x_im, m):
    out = product(m, halves(jnp.concatenate([x_re, x_im], 0)), NN)
    return out[:LANES], out[LANES:]


def exchange(blocks):
    blocks = list(blocks)
    lane = lax.broadcasted_iota(jnp.int32, blocks[0].shape, 1)
    for bit, shift in ((4, 64), (2, 32), (1, 16)):
        low = (lane & shift) == 0
        for k in range(8):
            if k & bit == 0:
                a, b = blocks[k], blocks[k | bit]
                t = jnp.where(low, b, a)
                t = pltpu.roll(t, 64, 1) if shift == 64 else jnp.take_along_axis(t, lane ^ shift, axis=1)
                blocks[k] = jnp.where(low, a, t)
                blocks[k | bit] = jnp.where(low, t, b)
    return blocks


def high_gate(s, m):
    for pair in range(2):
        bs = (2 * pair, 2 * pair + 1)
        x = [jnp.concatenate([s[c, pl.ds(b, LANES, stride=4), :] for b in bs], 1) for c in range(2)]
        y = left_gate(*x, m)
        for c in range(2):
            for k, b in enumerate(bs):
                s[c, pl.ds(b, LANES, stride=4), :] = y[c][:, k * LANES : (k + 1) * LANES]


def upper_gate(s, m, store):
    for pair in range(2):
        bs = (2 * pair, 2 * pair + 1)
        x = [jnp.concatenate([s[c, pl.ds(b * LANES, LANES), :] for b in bs], 1) for c in range(2)]
        y = left_gate(*x, m)
        for c in range(2):
            for k, b in enumerate(bs):
                store(c, b * LANES, y[c][:, k * LANES : (k + 1) * LANES])


def middle_gate(s, m):
    count = s.shape[1] // LANES
    for first in range(0, count, 2):
        bs = tuple(range(first, min(first + 2, count)))
        x = [
            jnp.concatenate(
                [
                    jnp.concatenate(exchange([s[c, pl.ds(b * LANES + 16 * k, 16), :] for k in range(8)]), 0)
                    for b in bs
                ],
                1,
            )
            for c in range(2)
        ]
        y = left_gate(*x, m)
        for c in range(2):
            for n, b in enumerate(bs):
                part = y[c][:, n * LANES : (n + 1) * LANES]
                back = exchange([part[16 * k : 16 * k + 16] for k in range(8)])
                s[c, pl.ds(b * LANES, LANES), :] = jnp.concatenate(back, 0)


def low_gate(s, m):
    count = s.shape[1]
    for first in range(0, count, PAIR):
        at = pl.ds(first, min(PAIR, count - first))
        y = right_gate(s[0, at, :], s[1, at, :], m)
        for c in range(2):
            s[c, at, :] = y[c]


def keeper(s):
    def store(c, row, value):
        s[c, pl.ds(row, LANES), :] = value

    return store


def reversed3(v):
    return ((v & 1) << 2) | (v & 2) | ((v >> 2) & 1)


def rows_of(block, size):
    return pl.ds(pl.multiple_of(block * size, size), size)


def split(ref):
    return ref.at[0], ref.at[1]


class Gates:
    def __init__(self, source, scratch, indices):
        self.own, self.sems, self.mh, self.ml = scratch
        self.indices = indices
        self.copies = [
            pltpu.make_async_copy(source.at[:, g], self.own.at[k], self.sems.at[k]) for k, g in enumerate(indices)
        ]

    def start(self, ks):
        for k in ks:
            self.copies[k].start()

    def ready(self, ks):
        for k in ks:
            self.copies[k].wait()
        for k in ks:
            prepare(self.own.at[k], self.indices[k] % 4 == 1, self.mh.at[k], self.ml.at[k])

    def __getitem__(self, g):
        k = self.indices.index(g)
        return self.mh[k], self.ml[k]


class Given:
    def __init__(self, mh, ml, indices):
        self.mh, self.ml, self.indices = mh, ml, indices

    def __getitem__(self, g):
        k = self.indices.index(g)
        return self.mh[k], self.ml[k]


def prepare_all(source, indices, mh, ml):
    for k, g in enumerate(indices):
        prepare(source.at[:, g], g % 4 == 1, mh.at[k], ml.at[k])


class Ready:
    def __init__(self, source, scratch, indices):
        self.mh, self.ml = scratch
        self.indices = indices
        prepare_all(source, indices, self.mh, self.ml)

    def __getitem__(self, g):
        k = self.indices.index(g)
        return self.mh[k], self.ml[k]


def first_kernel(indices, me_ref, amps, gates, q2, q1, own3, own0, give, s, own, sems, mh, ml, x, xsems):
    g = Gates(gates, (own, sems, mh, ml), indices)
    parts = []
    for b in range(2):
        at = pl.ds(2 * PAIR * b, 2 * PAIR)
        parts.append(pltpu.make_async_copy(amps.at[at], x.at[at], xsems.at[b]))
    g.start([0])
    for copy in parts:
        copy.start()
    g.start(range(1, len(indices)))
    low3 = me_ref[0] & 7
    g.ready([0])
    for b in range(2):
        parts[b].wait()
        y = right_gate(*[x[pl.ds(2 * PAIR * b + c, PAIR, stride=2), :] for c in range(2)], g[0])
        for c in range(2):
            s[c, pl.ds(b * PAIR, PAIR), :] = y[c]
    g.ready(range(1, len(indices)))
    middle_gate(s, g[1])
    high_gate(s, g[2])
    upper_gate(s, g[3], keeper(s))
    for mask, out in enumerate((own0, give.at[0], *split(q1), *split(q2), own3, give.at[1])):
        at = rows_of(reversed3(low3 ^ mask), 64)
        for c in range(2):
            out[c] = s[c, at, :]


def lower_blocks(s, g, blocks, outs):
    for n, block in enumerate(blocks):
        for c in range(2):
            s[c, pl.ds(64 * n, 64), :] = block[c]
    low_gate(s, g[4])
    middle_gate(s, g[5])
    low_gate(s, g[8])
    for n, out in enumerate(outs):
        for c in range(2):
            out[c] = s[c, pl.ds(64 * n, 64), :]


def before_lower(indices, own0, own3, recv, gates, p0, p3, s, mh, ml):
    g = Ready(gates, (mh, ml), indices)
    lower_blocks(s, g, (own0, recv.at[0], own3, recv.at[1]), (*split(p0), *split(p3)))


def after_lower(indices, r1, r2, gates, keep, send1, send2, wh, wl, s, mh, ml):
    prepare_all(gates, (6, 7), wh, wl)
    g = Ready(gates, (mh, ml), indices)
    lower_blocks(s, g, (*split(r1), *split(r2)), (keep.at[0], send1, keep.at[1], send2))


def second_kernel(indices, me_ref, p0, near, r3, post1, post2, wh, wl, own, give, y1, self0, s, mh, ml):
    g = Given(wh, wl, indices)
    me = me_ref[0]
    low3, core = me & 7, me & 1
    blocks = (*split(p0), near.at[0], post1, near.at[1], post2, *split(r3))
    for mask, block in enumerate(blocks):
        at = rows_of(reversed3(low3 ^ mask), 64)
        for c in range(2):
            s[c, at, :] = block[c]
    high_gate(s, g[6])
    upper_gate(s, g[7], keeper(s))

    def write(out, mask):
        at = rows_of(me ^ mask, 32)
        for c in range(2):
            out[c] = s[c, at, :]

    for i, base in enumerate(PORTS):
        for f in range(2):
            write(own.at[i, f], 2 * (base + core) + f)
            write(give.at[2 * i + f], 2 * (base + 1 - core) + (1 - f))
    write(give.at[6], 3)
    write(give.at[7], 1)
    write(y1, 2)
    write(self0, 0)


def gate_nine(s, g, blocks, outs):
    for n, block in enumerate(blocks):
        for c in range(2):
            s[c, pl.ds(32 * n, 32), :] = block[c]
    middle_gate(s, g[9])
    for n, out in enumerate(outs):
        for c in range(2):
            out[c] = s[c, pl.ds(32 * n, 32), :]


def before_kernel(indices, own, recv, gates, out0, out1, s, mh, ml):
    g = Ready(gates, (mh, ml), indices)
    gate_nine(s, g, (*split(own), *split(recv)), [out.at[src] for src in range(2) for out in (out0, out1)])


def after_kernel(indices, a0, a1, y1, self0, other, gates, keep, send, wh, wl, s, mh, ml):
    prepare_all(gates, (10, 11), wh, wl)
    g = Ready(gates, (mh, ml), indices)
    blocks = [a.at[f, src] for f in range(2) for a in (a0, a1) for src in range(2)]
    blocks = blocks[:4] + [y1.at[0], y1.at[1], self0, other] + blocks[4:]
    gate_nine(s, g, blocks, [keep.at[n] for n in range(8)] + [send.at[n] for n in range(4)])


def join_kernel(indices, mine, late, out, s, mh, ml):
    for n, block in enumerate((*split(mine), *split(late))):
        for c in range(2):
            out[n, c] = block[c]


def third_kernel(indices, me_ref, keep, early, far, wh, wl, out, s, mh, ml, y, ysems):
    g = Given(wh, wl, indices)
    me = me_ref[0]
    core = me & 1

    def place(block, mask):
        at = rows_of(me ^ mask, 32)
        for c in range(2):
            s[c, at, :] = block[c]

    for i, base in enumerate(PORTS):
        for src in range(2):
            place(keep.at[2 * i + src] if i < 2 else far.at[src], 2 * (base + core) + src)
            place(early.at[2 * i + src] if i < 2 else far.at[2 + src], 2 * (base + 1 - core) + (1 - src))
    for n, mask in ((4, 2), (5, 3), (6, 0), (7, 1)):
        place(keep.at[n], mask)
    high_gate(s, g[10])
    copies = []

    def store(c, row, value):
        y[pl.ds(2 * row + c, LANES, stride=2), :] = value
        if c == 1 and row % PAIR == LANES:
            at = pl.ds(2 * (row - LANES), 2 * PAIR)
            copies.append(pltpu.make_async_copy(y.at[at], out.at[at], ysems.at[len(copies)]))
            copies[-1].start()

    upper_gate(s, g[11], store)
    for copy in copies:
        copy.wait()


def shape(*dims):
    return jax.ShapeDtypeStruct(dims, F32)


COST = {name: pl.CostEstimate(flops=n, bytes_accessed=1 << 18, transcendentals=0) for name, n in {"join_kernel": 2000000000, "after_kernel": 2000000000, "after_lower": 2000000000, "before_kernel": 1000000000, "before_lower": 2000000000}.items()}


def call(kernel, indices, outs, rows, operands, specs, scratch=(), out_specs=None, limit=32 << 20):
    n = len(indices)
    fetch = [pltpu.VMEM((n, 2, LANES, LANES), F32), pltpu.SemaphoreType.DMA((n,))] if specs[-1] is HBM else []
    return pl.pallas_call(
        functools.partial(kernel, indices),
        out_shape=outs,
        in_specs=specs,
        out_specs=out_specs or [VMEM] * len(outs),
        scratch_shapes=[
            pltpu.VMEM((2, rows, LANES), F32),
            *fetch,
            pltpu.VMEM((n, PAIR, PAIR), BF16),
            pltpu.VMEM((n, PAIR, PAIR), BF16),
            *scratch,
        ],
        compiler_params=pltpu.CompilerParams(vmem_limit_bytes=limit),
        name=kernel.__name__,
        cost_estimate=COST.get(kernel.__name__),
    )(*operands)


def flipped(block, mask, port=0):
    route = [(i, i ^ mask ^ (port if i & 1 else 0)) for i in range(lax.axis_size("node"))]
    return lax.ppermute(block, "node", route)


def fast_body(amplitudes, gates):
    total = amplitudes.shape[1]
    rows = total // LANES
    eighth, part16 = rows // 8, rows // 16
    me = lax.axis_index("node").astype(jnp.int32).reshape(1)
    x = amplitudes.reshape(2, rows, LANES).transpose(1, 0, 2).reshape(2 * rows, LANES)
    interleaved = (pltpu.VMEM((2 * rows, LANES), F32), pltpu.SemaphoreType.DMA((2,)))
    one, two = shape(2, eighth, LANES), shape(2, 2, eighth, LANES)
    q2, q1, own3, own0, give = call(
        first_kernel,
        (0, 1, 2, 3),
        [two, two, one, one, two],
        rows,
        [me, x, gates],
        [SMEM, HBM, HBM],
        interleaved,
        limit=532 * 104858,
    )
    recv = flipped(give, 1)
    r1, r2 = flipped(q1, 2), flipped(q2, 4)
    p0, p3 = call(before_lower, (4, 5, 8), [two, two], 4 * eighth, [own0, own3, recv, gates], [VMEM] * 4)
    r3 = flipped(p3, 6)
    weights = [jax.ShapeDtypeStruct((2, PAIR, PAIR), BF16)] * 2
    near, send1, send2, *w = call(after_lower, (4, 5, 8), [two, one, one, *weights], 4 * eighth, [r1, r2, gates], [VMEM] * 3)
    post1, post2 = flipped(send1, 1), flipped(send2, 1)
    block = (2, part16, LANES)
    own, give, y1, self0 = call(
        second_kernel,
        (6, 7),
        [shape(3, 2, *block), shape(8, *block), shape(*block), shape(*block)],
        rows,
        [me, p0, near, r3, post1, post2, *w],
        [SMEM] + [VMEM] * 7,
    )
    recv = flipped(give, 1)
    ready = call(
        before_kernel, (9,), [shape(2, *block)] * 2, 4 * part16, [own[2], recv[4:6], gates], [VMEM] * 3
    )
    payloads = [jnp.stack([own[i], recv[2 * i : 2 * i + 2]], 1) for i in range(2)]
    a0, a1 = [flipped(payload, 2 * base, 2) for base, payload in zip(PORTS, payloads)]
    mine, late = [flipped(payload, 2 * PORTS[2] + f, 2) for f, payload in enumerate(ready)]
    y1 = flipped(jnp.stack([y1, recv[6]]), 2)
    keep, send, *w = call(
        after_kernel,
        (9,),
        [shape(8, *block), shape(4, *block), *weights],
        12 * part16,
        [a0, a1, y1, self0, recv[7], gates],
        [VMEM] * 6,
    )
    early = flipped(send, 1)
    far = call(join_kernel, (9,), [shape(4, *block)], 8, [mine, late], [VMEM] * 2)[0]
    out = call(
        third_kernel,
        (10, 11),
        [shape(2 * rows, LANES)],
        rows,
        [me, keep, early, far, *w],
        [SMEM] + [VMEM] * 5,
        interleaved,
        [HBM],
    )[0]
    return out.reshape(rows, 2, LANES).transpose(1, 0, 2).reshape(2, total)


def swapped(block, axis, apart):
    count = lax.axis_size(axis)
    route = []
    for low in range(count):
        high = low | 1 << apart
        if high != low and high < count:
            route += [(low, high), (high, low)]
    return lax.ppermute(block, axis, route)


def apply_gate(state, gate_pair, offset):
    total = state.shape[1]
    real_g, imag_g = (gate_pair[0], gate_pair[1])
    hp = lax.Precision.HIGHEST
    if offset == 0:
        view = state.reshape(2, total // 128, 128)
        real_in, imag_in = (view[0], view[1])
        real_out = jnp.einsum("ij,aj->ai", real_g, real_in, precision=hp) - jnp.einsum(
            "ij,aj->ai", imag_g, imag_in, precision=hp
        )
        imag_out = jnp.einsum("ij,aj->ai", real_g, imag_in, precision=hp) + jnp.einsum(
            "ij,aj->ai", imag_g, real_in, precision=hp
        )
        return jnp.stack([real_out, imag_out], 0).reshape(2, total)
    inner = 1 << offset
    outer = total // (128 * inner)
    folded = 1
    if inner < 128:
        folded = min(128 // inner, outer)
    view = state.reshape(2, outer // folded, folded, 128, inner)
    view = jnp.transpose(view, (0, 1, 3, 2, 4)).reshape(2, outer // folded, 128, folded * inner)
    real_in, imag_in = (view[0], view[1])
    real_out = jnp.einsum("ij,ajb->aib", real_g, real_in, precision=hp) - jnp.einsum(
        "ij,ajb->aib", imag_g, imag_in, precision=hp
    )
    imag_out = jnp.einsum("ij,ajb->aib", real_g, imag_in, precision=hp) + jnp.einsum(
        "ij,ajb->aib", imag_g, real_in, precision=hp
    )
    result = jnp.stack([real_out, imag_out], 0).reshape(2, outer // folded, 128, folded, inner)
    return jnp.transpose(result, (0, 1, 3, 2, 4)).reshape(2, total)


def run_gates(state, gates, indices, offsets):
    distinct = gates.shape[1]
    for index, offset in zip(indices, offsets):
        state = apply_gate(state, gates[:, index % distinct], offset)
    return state


def leave_alone(half):
    return half


def split_halves(state, position, bit):
    total = state.shape[1]
    mine = lax.axis_index("node") // (1 << bit) % 2
    view = state.reshape(2, total >> position + 1, 2, 1 << position)
    keep = lax.dynamic_index_in_dim(view, mine, 2, keepdims=False)
    other = lax.dynamic_index_in_dim(view, 1 - mine, 2, keepdims=False)
    return (mine, keep, other)


def join_halves(mine, keep, arrived, total):
    lower = jnp.where(mine == 0, keep, arrived)
    upper = jnp.where(mine == 0, arrived, keep)
    return jnp.stack([lower, upper], 2).reshape(2, total)


def enter_bit(state, position, bit, prepare):
    total = state.shape[1]
    mine, keep, other = split_halves(state, position, bit)
    other = prepare(other.reshape(2, total // 2)).reshape(keep.shape)
    arrived = swapped(other, "node", bit)
    keep = prepare(keep.reshape(2, total // 2)).reshape(arrived.shape)
    return join_halves(mine, keep, arrived, total)


def general_body(amplitudes, gates):
    total = amplitudes.shape[1]
    locq = total.bit_length() - 1
    devices_node = lax.axis_size("node")
    offsets = [0, (locq - 7) // 2, locq - 7, locq - 9]
    state = run_gates(amplitudes, gates, [0, 1, 2, 3], offsets)

    def early_gates(half):
        return run_gates(half, gates, [4, 5], offsets[:2])

    state = enter_bit(state, locq - 1, 0, early_gates)
    for bit in range(1, 3):
        state = enter_bit(state, locq - 1 - bit, bit, leave_alone)
    state = run_gates(state, gates, [6, 7], offsets[2:])
    blocks = state.reshape(2, devices_node, total // devices_node)
    blocks = lax.all_to_all(blocks, "node", split_axis=1, concat_axis=1, tiled=True)
    state = blocks.reshape(2, total)
    return run_gates(state, gates, [8, 9, 10, 11], offsets)


def body(amplitudes, gates):
    if amplitudes.shape[1] == 65536 and lax.axis_size("node") == 16 and gates.shape[1] == 12:
        return fast_body(amplitudes, gates)
    return general_body(amplitudes, gates)


def solution(mesh):
    in_specs = (P(None, ("paths", "node")), P())
    out_specs = P(None, ("paths", "node"))
    return jax.shard_map(body, mesh=mesh, in_specs=in_specs, out_specs=out_specs, check_vma=False)
```

```python
import functools

import jax
import jax.numpy as jnp
from jax import lax
from jax.experimental import pallas as pl
from jax.experimental.pallas import tpu as pltpu
from jax.sharding import PartitionSpec as P

F32, BF16 = jnp.float32, jnp.bfloat16
LANES = 128
PAIR = 2 * LANES
NT = (((1,), (1,)), ((), ()))
NN = (((1,), (0,)), ((), ()))
PORTS = (4, 2, 6)
SMEM = pl.BlockSpec(memory_space=pltpu.SMEM)
VMEM = pl.BlockSpec(memory_space=pltpu.VMEM)
ANY = pl.BlockSpec(memory_space=pl.ANY)
HBM = pl.BlockSpec(memory_space=pltpu.HBM)


def halves(x):
    high = x.astype(BF16)
    return high, (x - high.astype(F32)).astype(BF16)


def product(a, b, dims):
    (ah, al), (bh, bl) = a, b
    dot = functools.partial(lax.dot_general, dimension_numbers=dims, preferred_element_type=F32)
    return dot(ah, bh) + (dot(al, bh) + dot(ah, bl))


def natural_gate(g):
    return g[0], g[1]


def regrouped_gate(g):
    order = lax.broadcasted_iota(jnp.int32, (LANES, LANES), 1)
    order = (order % 16) * 8 + order // 16
    out = []
    for c in range(2):
        rows = jnp.concatenate([g[c, pl.ds(m, 16, stride=8), :] for m in range(8)], 0)
        out.append(jnp.take_along_axis(rows, order, axis=1))
    return out


def prepare(g, regroup, mh, ml):
    re, im = regrouped_gate(g) if regroup else natural_gate(g)
    for r, row in enumerate(((re, -im), (im, re))):
        for c, part in enumerate(row):
            high, low = halves(part)
            at = (pl.ds(r * LANES, LANES), pl.ds(c * LANES, LANES))
            mh[at] = high
            ml[at] = low


def right_gate(x_re, x_im, m):
    out = product(halves(jnp.concatenate([x_re, x_im], 1)), m, NT)
    return out[:, :LANES], out[:, LANES:]


def left_gate(x_re, x_im, m):
    out = product(m, halves(jnp.concatenate([x_re, x_im], 0)), NN)
    return out[:LANES], out[LANES:]


def exchange(blocks):
    blocks = list(blocks)
    lane = lax.broadcasted_iota(jnp.int32, blocks[0].shape, 1)
    for bit, shift in ((4, 64), (2, 32), (1, 16)):
        low = (lane & shift) == 0
        for k in range(8):
            if k & bit == 0:
                a, b = blocks[k], blocks[k | bit]
                t = jnp.where(low, b, a)
                t = pltpu.roll(t, 64, 1) if shift == 64 else jnp.take_along_axis(t, lane ^ shift, axis=1)
                blocks[k] = jnp.where(low, a, t)
                blocks[k | bit] = jnp.where(low, t, b)
    return blocks


def high_gate(s, m):
    for pair in range(2):
        bs = (2 * pair, 2 * pair + 1)
        x = [jnp.concatenate([s[c, pl.ds(b, LANES, stride=4), :] for b in bs], 1) for c in range(2)]
        y = left_gate(*x, m)
        for c in range(2):
            for k, b in enumerate(bs):
                s[c, pl.ds(b, LANES, stride=4), :] = y[c][:, k * LANES : (k + 1) * LANES]


def upper_gate(s, m, store):
    for pair in range(2):
        bs = (2 * pair, 2 * pair + 1)
        x = [jnp.concatenate([s[c, pl.ds(b * LANES, LANES), :] for b in bs], 1) for c in range(2)]
        y = left_gate(*x, m)
        for c in range(2):
            for k, b in enumerate(bs):
                store(c, b * LANES, y[c][:, k * LANES : (k + 1) * LANES])


def middle_gate(s, m):
    count = s.shape[1] // LANES
    for first in range(0, count, 2):
        bs = tuple(range(first, min(first + 2, count)))
        x = [
            jnp.concatenate(
                [
                    jnp.concatenate(exchange([s[c, pl.ds(b * LANES + 16 * k, 16), :] for k in range(8)]), 0)
                    for b in bs
                ],
                1,
            )
            for c in range(2)
        ]
        y = left_gate(*x, m)
        for c in range(2):
            for n, b in enumerate(bs):
                part = y[c][:, n * LANES : (n + 1) * LANES]
                back = exchange([part[16 * k : 16 * k + 16] for k in range(8)])
                s[c, pl.ds(b * LANES, LANES), :] = jnp.concatenate(back, 0)


def low_gate(s, m):
    count = s.shape[1]
    for first in range(0, count, PAIR):
        at = pl.ds(first, min(PAIR, count - first))
        y = right_gate(s[0, at, :], s[1, at, :], m)
        for c in range(2):
            s[c, at, :] = y[c]


def keeper(s):
    def store(c, row, value):
        s[c, pl.ds(row, LANES), :] = value

    return store


def reversed3(v):
    return ((v & 1) << 2) | (v & 2) | ((v >> 2) & 1)


def rows_of(block, size):
    return pl.ds(pl.multiple_of(block * size, size), size)


def split(ref):
    return ref.at[0], ref.at[1]


class Gates:
    def __init__(self, source, scratch, indices):
        self.own, self.sems, self.mh, self.ml = scratch
        self.indices = indices
        self.copies = [
            pltpu.make_async_copy(source.at[:, g], self.own.at[k], self.sems.at[k]) for k, g in enumerate(indices)
        ]

    def start(self, ks):
        for k in ks:
            self.copies[k].start()

    def ready(self, ks):
        for k in ks:
            self.copies[k].wait()
        for k in ks:
            prepare(self.own.at[k], self.indices[k] % 4 == 1, self.mh.at[k], self.ml.at[k])

    def __getitem__(self, g):
        k = self.indices.index(g)
        return self.mh[k], self.ml[k]


class Given:
    def __init__(self, mh, ml, indices):
        self.mh, self.ml, self.indices = mh, ml, indices

    def __getitem__(self, g):
        k = self.indices.index(g)
        return self.mh[k], self.ml[k]


def prepare_all(source, indices, mh, ml):
    for k, g in enumerate(indices):
        prepare(source.at[:, g], g % 4 == 1, mh.at[k], ml.at[k])


class Ready:
    def __init__(self, source, scratch, indices):
        self.mh, self.ml = scratch
        self.indices = indices
        prepare_all(source, indices, self.mh, self.ml)

    def __getitem__(self, g):
        k = self.indices.index(g)
        return self.mh[k], self.ml[k]


def first_kernel(indices, me_ref, amps, gates, q2, q1, own3, own0, give, s, own, sems, mh, ml, x, xsems):
    g = Gates(gates, (own, sems, mh, ml), indices)
    parts = []
    for b in range(2):
        at = pl.ds(2 * PAIR * b, 2 * PAIR)
        parts.append(pltpu.make_async_copy(amps.at[at], x.at[at], xsems.at[b]))
    g.start([0])
    for copy in parts:
        copy.start()
    g.start(range(1, len(indices)))
    low3 = me_ref[0] & 7
    g.ready([0])
    for b in range(2):
        parts[b].wait()
        y = right_gate(*[x[pl.ds(2 * PAIR * b + c, PAIR, stride=2), :] for c in range(2)], g[0])
        for c in range(2):
            s[c, pl.ds(b * PAIR, PAIR), :] = y[c]
    g.ready(range(1, len(indices)))
    middle_gate(s, g[1])
    high_gate(s, g[2])
    upper_gate(s, g[3], keeper(s))
    for mask, out in enumerate((own0, give.at[0], *split(q1), *split(q2), own3, give.at[1])):
        at = rows_of(reversed3(low3 ^ mask), 64)
        for c in range(2):
            out[c] = s[c, at, :]


def lower_blocks(s, g, blocks, outs):
    for n, block in enumerate(blocks):
        for c in range(2):
            s[c, pl.ds(64 * n, 64), :] = block[c]
    low_gate(s, g[4])
    middle_gate(s, g[5])
    low_gate(s, g[8])
    for n, out in enumerate(outs):
        for c in range(2):
            out[c] = s[c, pl.ds(64 * n, 64), :]


def before_lower(indices, own0, own3, recv, gates, p0, p3, s, mh, ml):
    g = Ready(gates, (mh, ml), indices)
    lower_blocks(s, g, (own0, recv.at[0], own3, recv.at[1]), (*split(p0), *split(p3)))


def after_lower(indices, r1, r2, gates, keep, send1, send2, wh, wl, s, mh, ml):
    prepare_all(gates, (6, 7), wh, wl)
    g = Ready(gates, (mh, ml), indices)
    lower_blocks(s, g, (*split(r1), *split(r2)), (keep.at[0], send1, keep.at[1], send2))


def second_kernel(indices, me_ref, p0, near, r3, post1, post2, wh, wl, own, give, y1, self0, s, mh, ml):
    g = Given(wh, wl, indices)
    me = me_ref[0]
    low3, core = me & 7, me & 1
    blocks = (*split(p0), near.at[0], post1, near.at[1], post2, *split(r3))
    for mask, block in enumerate(blocks):
        at = rows_of(reversed3(low3 ^ mask), 64)
        for c in range(2):
            s[c, at, :] = block[c]
    high_gate(s, g[6])
    upper_gate(s, g[7], keeper(s))

    def write(out, mask):
        at = rows_of(me ^ mask, 32)
        for c in range(2):
            out[c] = s[c, at, :]

    for i, base in enumerate(PORTS):
        for f in range(2):
            write(own.at[i, f], 2 * (base + core) + f)
            write(give.at[2 * i + f], 2 * (base + 1 - core) + (1 - f))
    write(give.at[6], 3)
    write(give.at[7], 1)
    write(y1, 2)
    write(self0, 0)


def gate_nine(s, g, blocks, outs):
    for n, block in enumerate(blocks):
        for c in range(2):
            s[c, pl.ds(32 * n, 32), :] = block[c]
    middle_gate(s, g[9])
    for n, out in enumerate(outs):
        for c in range(2):
            out[c] = s[c, pl.ds(32 * n, 32), :]


def before_kernel(indices, own, recv, gates, out0, out1, s, mh, ml):
    g = Ready(gates, (mh, ml), indices)
    gate_nine(s, g, (*split(own), *split(recv)), [out.at[src] for src in range(2) for out in (out0, out1)])


def after_kernel(indices, a0, a1, y1, self0, other, gates, keep, send, wh, wl, s, mh, ml):
    prepare_all(gates, (10, 11), wh, wl)
    g = Ready(gates, (mh, ml), indices)
    blocks = [a.at[f, src] for f in range(2) for a in (a0, a1) for src in range(2)]
    blocks = blocks[:4] + [y1.at[0], y1.at[1], self0, other] + blocks[4:]
    gate_nine(s, g, blocks, [keep.at[n] for n in range(8)] + [send.at[n] for n in range(4)])


def join_kernel(indices, late, mine, out, s, mh, ml):
    for n, block in enumerate((*split(mine), *split(late))):
        for c in range(2):
            out[n, c] = block[c]


def third_kernel(indices, me_ref, keep, early, far, wh, wl, out, s, mh, ml, y, ysems):
    g = Given(wh, wl, indices)
    me = me_ref[0]
    core = me & 1

    def place(block, mask):
        at = rows_of(me ^ mask, 32)
        for c in range(2):
            s[c, at, :] = block[c]

    for i, base in enumerate(PORTS):
        for src in range(2):
            place(keep.at[2 * i + src] if i < 2 else far.at[src], 2 * (base + core) + src)
            place(early.at[2 * i + src] if i < 2 else far.at[2 + src], 2 * (base + 1 - core) + (1 - src))
    for n, mask in ((4, 2), (5, 3), (6, 0), (7, 1)):
        place(keep.at[n], mask)
    high_gate(s, g[10])
    copies = []

    def store(c, row, value):
        y[pl.ds(2 * row + c, LANES, stride=2), :] = value
        if c == 1 and row % PAIR == LANES:
            at = pl.ds(2 * (row - LANES), 2 * PAIR)
            copies.append(pltpu.make_async_copy(y.at[at], out.at[at], ysems.at[len(copies)]))
            copies[-1].start()

    upper_gate(s, g[11], store)
    for copy in copies:
        copy.wait()


def shape(*dims):
    return jax.ShapeDtypeStruct(dims, F32)


COST = {name: pl.CostEstimate(flops=n, bytes_accessed=1 << 18, transcendentals=0) for name, n in {"join_kernel": 2000000000, "after_kernel": 2000000000, "after_lower": 2000000000, "before_kernel": 1000000000, "before_lower": 2000000000}.items()}


def call(kernel, indices, outs, rows, operands, specs, scratch=(), out_specs=None, limit=32 << 20):
    n = len(indices)
    fetch = [pltpu.VMEM((n, 2, LANES, LANES), F32), pltpu.SemaphoreType.DMA((n,))] if specs[-1] is HBM else []
    return pl.pallas_call(
        functools.partial(kernel, indices),
        out_shape=outs,
        in_specs=specs,
        out_specs=out_specs or [VMEM] * len(outs),
        scratch_shapes=[
            pltpu.VMEM((2, rows, LANES), F32),
            *fetch,
            pltpu.VMEM((n, PAIR, PAIR), BF16),
            pltpu.VMEM((n, PAIR, PAIR), BF16),
            *scratch,
        ],
        compiler_params=pltpu.CompilerParams(vmem_limit_bytes=limit),
        name=kernel.__name__,
        cost_estimate=COST.get(kernel.__name__),
    )(*operands)


def flipped(block, mask, port=0):
    route = [(i, i ^ mask ^ (port if i & 1 else 0)) for i in range(lax.axis_size("node"))]
    return lax.ppermute(block, "node", route)


def fast_body(amplitudes, gates):
    total = amplitudes.shape[1]
    rows = total // LANES
    eighth, part16 = rows // 8, rows // 16
    me = lax.axis_index("node").astype(jnp.int32).reshape(1)
    x = amplitudes.reshape(2, rows, LANES).transpose(1, 0, 2).reshape(2 * rows, LANES)
    interleaved = (pltpu.VMEM((2 * rows, LANES), F32), pltpu.SemaphoreType.DMA((2,)))
    one, two = shape(2, eighth, LANES), shape(2, 2, eighth, LANES)
    q2, q1, own3, own0, give = call(
        first_kernel,
        (0, 1, 2, 3),
        [two, two, one, one, two],
        rows,
        [me, x, gates],
        [SMEM, HBM, HBM],
        interleaved,
        limit=532 * 104858,
    )
    recv = flipped(give, 1)
    r1, r2 = flipped(q1, 2), flipped(q2, 4)
    p0, p3 = call(before_lower, (4, 5, 8), [two, two], 4 * eighth, [own0, own3, recv, gates], [VMEM] * 4)
    r3 = flipped(p3, 6)
    weights = [jax.ShapeDtypeStruct((2, PAIR, PAIR), BF16)] * 2
    near, send1, send2, *w = call(after_lower, (4, 5, 8), [two, one, one, *weights], 4 * eighth, [r1, r2, gates], [VMEM] * 3)
    post1, post2 = flipped(send1, 1), flipped(send2, 1)
    block = (2, part16, LANES)
    own, give, y1, self0 = call(
        second_kernel,
        (6, 7),
        [shape(3, 2, *block), shape(8, *block), shape(*block), shape(*block)],
        rows,
        [me, p0, near, r3, post1, post2, *w],
        [SMEM] + [VMEM] * 7,
    )
    recv = flipped(give, 1)
    ready = call(
        before_kernel, (9,), [shape(2, *block)] * 2, 4 * part16, [own[2], recv[4:6], gates], [VMEM] * 3
    )
    payloads = [jnp.stack([own[i], recv[2 * i : 2 * i + 2]], 1) for i in range(2)]
    a0, a1 = [flipped(payload, 2 * base, 2) for base, payload in zip(PORTS, payloads)]
    mine, late = [flipped(payload, 2 * PORTS[2] + f, 2) for f, payload in enumerate(ready)]
    y1 = flipped(jnp.stack([y1, recv[6]]), 2)
    keep, send, *w = call(
        after_kernel,
        (9,),
        [shape(8, *block), shape(4, *block), *weights],
        12 * part16,
        [a0, a1, y1, self0, recv[7], gates],
        [VMEM] * 6,
    )
    early = flipped(send, 1)
    far = call(join_kernel, (9,), [shape(4, *block)], 8, [late, mine], [VMEM] * 2)[0]
    out = call(
        third_kernel,
        (10, 11),
        [shape(2 * rows, LANES)],
        rows,
        [me, keep, early, far, *w],
        [SMEM] + [VMEM] * 5,
        interleaved,
        [HBM],
    )[0]
    return out.reshape(rows, 2, LANES).transpose(1, 0, 2).reshape(2, total)


def swapped(block, axis, apart):
    count = lax.axis_size(axis)
    route = []
    for low in range(count):
        high = low | 1 << apart
        if high != low and high < count:
            route += [(low, high), (high, low)]
    return lax.ppermute(block, axis, route)


def apply_gate(state, gate_pair, offset):
    total = state.shape[1]
    real_g, imag_g = (gate_pair[0], gate_pair[1])
    hp = lax.Precision.HIGHEST
    if offset == 0:
        view = state.reshape(2, total // 128, 128)
        real_in, imag_in = (view[0], view[1])
        real_out = jnp.einsum("ij,aj->ai", real_g, real_in, precision=hp) - jnp.einsum(
            "ij,aj->ai", imag_g, imag_in, precision=hp
        )
        imag_out = jnp.einsum("ij,aj->ai", real_g, imag_in, precision=hp) + jnp.einsum(
            "ij,aj->ai", imag_g, real_in, precision=hp
        )
        return jnp.stack([real_out, imag_out], 0).reshape(2, total)
    inner = 1 << offset
    outer = total // (128 * inner)
    folded = 1
    if inner < 128:
        folded = min(128 // inner, outer)
    view = state.reshape(2, outer // folded, folded, 128, inner)
    view = jnp.transpose(view, (0, 1, 3, 2, 4)).reshape(2, outer // folded, 128, folded * inner)
    real_in, imag_in = (view[0], view[1])
    real_out = jnp.einsum("ij,ajb->aib", real_g, real_in, precision=hp) - jnp.einsum(
        "ij,ajb->aib", imag_g, imag_in, precision=hp
    )
    imag_out = jnp.einsum("ij,ajb->aib", real_g, imag_in, precision=hp) + jnp.einsum(
        "ij,ajb->aib", imag_g, real_in, precision=hp
    )
    result = jnp.stack([real_out, imag_out], 0).reshape(2, outer // folded, 128, folded, inner)
    return jnp.transpose(result, (0, 1, 3, 2, 4)).reshape(2, total)


def run_gates(state, gates, indices, offsets):
    distinct = gates.shape[1]
    for index, offset in zip(indices, offsets):
        state = apply_gate(state, gates[:, index % distinct], offset)
    return state


def leave_alone(half):
    return half


def split_halves(state, position, bit):
    total = state.shape[1]
    mine = lax.axis_index("node") // (1 << bit) % 2
    view = state.reshape(2, total >> position + 1, 2, 1 << position)
    keep = lax.dynamic_index_in_dim(view, mine, 2, keepdims=False)
    other = lax.dynamic_index_in_dim(view, 1 - mine, 2, keepdims=False)
    return (mine, keep, other)


def join_halves(mine, keep, arrived, total):
    lower = jnp.where(mine == 0, keep, arrived)
    upper = jnp.where(mine == 0, arrived, keep)
    return jnp.stack([lower, upper], 2).reshape(2, total)


def enter_bit(state, position, bit, prepare):
    total = state.shape[1]
    mine, keep, other = split_halves(state, position, bit)
    other = prepare(other.reshape(2, total // 2)).reshape(keep.shape)
    arrived = swapped(other, "node", bit)
    keep = prepare(keep.reshape(2, total // 2)).reshape(arrived.shape)
    return join_halves(mine, keep, arrived, total)


def general_body(amplitudes, gates):
    total = amplitudes.shape[1]
    locq = total.bit_length() - 1
    devices_node = lax.axis_size("node")
    offsets = [0, (locq - 7) // 2, locq - 7, locq - 9]
    state = run_gates(amplitudes, gates, [0, 1, 2, 3], offsets)

    def early_gates(half):
        return run_gates(half, gates, [4, 5], offsets[:2])

    state = enter_bit(state, locq - 1, 0, early_gates)
    for bit in range(1, 3):
        state = enter_bit(state, locq - 1 - bit, bit, leave_alone)
    state = run_gates(state, gates, [6, 7], offsets[2:])
    blocks = state.reshape(2, devices_node, total // devices_node)
    blocks = lax.all_to_all(blocks, "node", split_axis=1, concat_axis=1, tiled=True)
    state = blocks.reshape(2, total)
    return run_gates(state, gates, [8, 9, 10, 11], offsets)


def body(amplitudes, gates):
    if amplitudes.shape[1] == 65536 and lax.axis_size("node") == 16 and gates.shape[1] == 12:
        return fast_body(amplitudes, gates)
    return general_body(amplitudes, gates)


def solution(mesh):
    in_specs = (P(None, ("paths", "node")), P())
    out_specs = P(None, ("paths", "node"))
    return jax.shard_map(body, mesh=mesh, in_specs=in_specs, out_specs=out_specs, check_vma=False)
```

```python
import functools

import jax
import jax.numpy as jnp
from jax import lax
from jax.experimental import pallas as pl
from jax.experimental.pallas import tpu as pltpu
from jax.sharding import PartitionSpec as P

F32, BF16 = jnp.float32, jnp.bfloat16
LANES = 128
PAIR = 2 * LANES
NT = (((1,), (1,)), ((), ()))
NN = (((1,), (0,)), ((), ()))
PORTS = (4, 2, 6)
SMEM = pl.BlockSpec(memory_space=pltpu.SMEM)
VMEM = pl.BlockSpec(memory_space=pltpu.VMEM)
ANY = pl.BlockSpec(memory_space=pl.ANY)
HBM = pl.BlockSpec(memory_space=pltpu.HBM)


def halves(x):
    high = x.astype(BF16)
    return high, (x - high.astype(F32)).astype(BF16)


def product(a, b, dims):
    (ah, al), (bh, bl) = a, b
    dot = functools.partial(lax.dot_general, dimension_numbers=dims, preferred_element_type=F32)
    return dot(ah, bh) + (dot(al, bh) + dot(ah, bl))


def natural_gate(g):
    return g[0], g[1]


def regrouped_gate(g):
    order = lax.broadcasted_iota(jnp.int32, (LANES, LANES), 1)
    order = (order % 16) * 8 + order // 16
    out = []
    for c in range(2):
        rows = jnp.concatenate([g[c, pl.ds(m, 16, stride=8), :] for m in range(8)], 0)
        out.append(jnp.take_along_axis(rows, order, axis=1))
    return out


def prepare(g, regroup, mh, ml):
    re, im = regrouped_gate(g) if regroup else natural_gate(g)
    for r, row in enumerate(((re, -im), (im, re))):
        for c, part in enumerate(row):
            high, low = halves(part)
            at = (pl.ds(r * LANES, LANES), pl.ds(c * LANES, LANES))
            mh[at] = high
            ml[at] = low


def right_gate(x_re, x_im, m):
    out = product(halves(jnp.concatenate([x_re, x_im], 1)), m, NT)
    return out[:, :LANES], out[:, LANES:]


def left_gate(x_re, x_im, m):
    out = product(m, halves(jnp.concatenate([x_re, x_im], 0)), NN)
    return out[:LANES], out[LANES:]


def exchange(blocks):
    blocks = list(blocks)
    lane = lax.broadcasted_iota(jnp.int32, blocks[0].shape, 1)
    for bit, shift in ((4, 64), (2, 32), (1, 16)):
        low = (lane & shift) == 0
        for k in range(8):
            if k & bit == 0:
                a, b = blocks[k], blocks[k | bit]
                t = jnp.where(low, b, a)
                t = pltpu.roll(t, 64, 1) if shift == 64 else jnp.take_along_axis(t, lane ^ shift, axis=1)
                blocks[k] = jnp.where(low, a, t)
                blocks[k | bit] = jnp.where(low, t, b)
    return blocks


def high_gate(s, m):
    for pair in range(2):
        bs = (2 * pair, 2 * pair + 1)
        x = [jnp.concatenate([s[c, pl.ds(b, LANES, stride=4), :] for b in bs], 1) for c in range(2)]
        y = left_gate(*x, m)
        for c in range(2):
            for k, b in enumerate(bs):
                s[c, pl.ds(b, LANES, stride=4), :] = y[c][:, k * LANES : (k + 1) * LANES]


def upper_gate(s, m, store):
    for pair in range(2):
        bs = (2 * pair, 2 * pair + 1)
        x = [jnp.concatenate([s[c, pl.ds(b * LANES, LANES), :] for b in bs], 1) for c in range(2)]
        y = left_gate(*x, m)
        for k, b in enumerate(bs):
            for c in range(2):
                store(c, b * LANES, y[c][:, k * LANES : (k + 1) * LANES])


def middle_gate(s, m):
    count = s.shape[1] // LANES
    for first in range(0, count, 2):
        bs = tuple(range(first, min(first + 2, count)))
        x = [
            jnp.concatenate(
                [
                    jnp.concatenate(exchange([s[c, pl.ds(b * LANES + 16 * k, 16), :] for k in range(8)]), 0)
                    for b in bs
                ],
                1,
            )
            for c in range(2)
        ]
        y = left_gate(*x, m)
        for c in range(2):
            for n, b in enumerate(bs):
                part = y[c][:, n * LANES : (n + 1) * LANES]
                back = exchange([part[16 * k : 16 * k + 16] for k in range(8)])
                s[c, pl.ds(b * LANES, LANES), :] = jnp.concatenate(back, 0)


def low_gate(s, m):
    count = s.shape[1]
    for first in range(0, count, PAIR):
        at = pl.ds(first, min(PAIR, count - first))
        y = right_gate(s[0, at, :], s[1, at, :], m)
        for c in range(2):
            s[c, at, :] = y[c]


def keeper(s):
    def store(c, row, value):
        s[c, pl.ds(row, LANES), :] = value

    return store


def reversed3(v):
    return ((v & 1) << 2) | (v & 2) | ((v >> 2) & 1)


def rows_of(block, size):
    return pl.ds(pl.multiple_of(block * size, size), size)


def split(ref):
    return ref.at[0], ref.at[1]


class Gates:
    def __init__(self, source, scratch, indices):
        self.own, self.sems, self.mh, self.ml = scratch
        self.indices = indices
        self.copies = [
            pltpu.make_async_copy(source.at[:, g], self.own.at[k], self.sems.at[k]) for k, g in enumerate(indices)
        ]

    def start(self, ks):
        for k in ks:
            self.copies[k].start()

    def ready(self, ks):
        for k in ks:
            self.copies[k].wait()
        for k in ks:
            prepare(self.own.at[k], self.indices[k] % 4 == 1, self.mh.at[k], self.ml.at[k])

    def __getitem__(self, g):
        k = self.indices.index(g)
        return self.mh[k], self.ml[k]


class Given:
    def __init__(self, mh, ml, indices):
        self.mh, self.ml, self.indices = mh, ml, indices

    def __getitem__(self, g):
        k = self.indices.index(g)
        return self.mh[k], self.ml[k]


def prepare_all(source, indices, mh, ml):
    for k, g in enumerate(indices):
        prepare(source.at[:, g], g % 4 == 1, mh.at[k], ml.at[k])


class Ready:
    def __init__(self, source, scratch, indices):
        self.mh, self.ml = scratch
        self.indices = indices
        prepare_all(source, indices, self.mh, self.ml)

    def __getitem__(self, g):
        k = self.indices.index(g)
        return self.mh[k], self.ml[k]


def first_kernel(indices, me_ref, amps, gates, q2, q1, own3, own0, give, s, own, sems, mh, ml, x, xsems):
    g = Gates(gates, (own, sems, mh, ml), indices)
    parts = []
    for b in range(2):
        at = pl.ds(2 * PAIR * b, 2 * PAIR)
        parts.append(pltpu.make_async_copy(amps.at[at], x.at[at], xsems.at[b]))
    g.start([0])
    for copy in parts:
        copy.start()
    g.start(range(1, len(indices)))
    low3 = me_ref[0] & 7
    g.ready([0])
    for b in range(2):
        parts[b].wait()
        y = right_gate(*[x[pl.ds(2 * PAIR * b + c, PAIR, stride=2), :] for c in range(2)], g[0])
        for c in range(2):
            s[c, pl.ds(b * PAIR, PAIR), :] = y[c]
    g.ready(range(1, len(indices)))
    middle_gate(s, g[1])
    high_gate(s, g[2])
    upper_gate(s, g[3], keeper(s))
    for mask, out in enumerate((own0, give.at[0], *split(q1), *split(q2), own3, give.at[1])):
        at = rows_of(reversed3(low3 ^ mask), 64)
        for c in range(2):
            out[c] = s[c, at, :]


def lower_blocks(s, g, blocks, outs):
    for n, block in enumerate(blocks):
        for c in range(2):
            s[c, pl.ds(64 * n, 64), :] = block[c]
    low_gate(s, g[4])
    middle_gate(s, g[5])
    low_gate(s, g[8])
    for n, out in enumerate(outs):
        for c in range(2):
            out[c] = s[c, pl.ds(64 * n, 64), :]


def before_lower(indices, own0, own3, recv, gates, p0, p3, s, mh, ml):
    g = Ready(gates, (mh, ml), indices)
    lower_blocks(s, g, (own0, recv.at[0], own3, recv.at[1]), (*split(p0), *split(p3)))


def after_lower(indices, r1, r2, gates, keep, send1, send2, wh, wl, s, mh, ml):
    prepare_all(gates, (6, 7), wh, wl)
    g = Ready(gates, (mh, ml), indices)
    lower_blocks(s, g, (*split(r1), *split(r2)), (keep.at[0], send1, keep.at[1], send2))


def second_kernel(indices, me_ref, p0, near, r3, post1, post2, wh, wl, own, give, y1, self0, s, mh, ml):
    g = Given(wh, wl, indices)
    me = me_ref[0]
    low3, core = me & 7, me & 1
    blocks = (*split(p0), near.at[0], post1, near.at[1], post2, *split(r3))
    for mask, block in enumerate(blocks):
        at = rows_of(reversed3(low3 ^ mask), 64)
        for c in range(2):
            s[c, at, :] = block[c]
    high_gate(s, g[6])
    upper_gate(s, g[7], keeper(s))

    def write(out, mask):
        at = rows_of(me ^ mask, 32)
        for c in range(2):
            out[c] = s[c, at, :]

    for i, base in enumerate(PORTS):
        for f in range(2):
            write(own.at[i, f], 2 * (base + core) + f)
            write(give.at[2 * i + f], 2 * (base + 1 - core) + (1 - f))
    write(give.at[6], 3)
    write(give.at[7], 1)
    write(y1, 2)
    write(self0, 0)


def gate_nine(s, g, blocks, outs):
    for n, block in enumerate(blocks):
        for c in range(2):
            s[c, pl.ds(32 * n, 32), :] = block[c]
    middle_gate(s, g[9])
    for n, out in enumerate(outs):
        for c in range(2):
            out[c] = s[c, pl.ds(32 * n, 32), :]


def before_kernel(indices, own, recv, gates, out0, out1, s, mh, ml):
    g = Ready(gates, (mh, ml), indices)
    gate_nine(s, g, (*split(own), *split(recv)), [out.at[src] for src in range(2) for out in (out0, out1)])


def after_kernel(indices, a0, a1, y1, self0, other, gates, keep, send, wh, wl, s, mh, ml):
    prepare_all(gates, (10, 11), wh, wl)
    g = Ready(gates, (mh, ml), indices)
    blocks = [a.at[f, src] for f in range(2) for a in (a0, a1) for src in range(2)]
    blocks = blocks[:4] + [y1.at[0], y1.at[1], self0, other] + blocks[4:]
    gate_nine(s, g, blocks, [keep.at[n] for n in range(8)] + [send.at[n] for n in range(4)])


def join_kernel(indices, mine, late, out, s, mh, ml):
    for n, block in enumerate((*split(mine), *split(late))):
        for c in range(2):
            out[n, c] = block[c]


def third_kernel(indices, me_ref, keep, early, far, wh, wl, out, s, mh, ml, y, ysems):
    g = Given(wh, wl, indices)
    me = me_ref[0]
    core = me & 1

    def place(block, mask):
        at = rows_of(me ^ mask, 32)
        for c in range(2):
            s[c, at, :] = block[c]

    for i, base in enumerate(PORTS):
        for src in range(2):
            place(keep.at[2 * i + src] if i < 2 else far.at[src], 2 * (base + core) + src)
            place(early.at[2 * i + src] if i < 2 else far.at[2 + src], 2 * (base + 1 - core) + (1 - src))
    for n, mask in ((4, 2), (5, 3), (6, 0), (7, 1)):
        place(keep.at[n], mask)
    high_gate(s, g[10])
    copies = []

    def store(c, row, value):
        y[pl.ds(2 * row + c, LANES, stride=2), :] = value
        if c == 1:
            at = pl.ds(2 * row, PAIR)
            copies.append(pltpu.make_async_copy(y.at[at], out.at[at], ysems.at[len(copies)]))
            copies[-1].start()

    upper_gate(s, g[11], store)
    for copy in copies:
        copy.wait()


def shape(*dims):
    return jax.ShapeDtypeStruct(dims, F32)


COST = {name: pl.CostEstimate(flops=n, bytes_accessed=1 << 18, transcendentals=0) for name, n in {"join_kernel": 2000000000, "after_kernel": 2000000000, "after_lower": 2000000000, "before_kernel": 1000000000, "before_lower": 2000000000}.items()}


def call(kernel, indices, outs, rows, operands, specs, scratch=(), out_specs=None, limit=32 << 20):
    n = len(indices)
    fetch = [pltpu.VMEM((n, 2, LANES, LANES), F32), pltpu.SemaphoreType.DMA((n,))] if specs[-1] is HBM else []
    return pl.pallas_call(
        functools.partial(kernel, indices),
        out_shape=outs,
        in_specs=specs,
        out_specs=out_specs or [VMEM] * len(outs),
        scratch_shapes=[
            pltpu.VMEM((2, rows, LANES), F32),
            *fetch,
            pltpu.VMEM((n, PAIR, PAIR), BF16),
            pltpu.VMEM((n, PAIR, PAIR), BF16),
            *scratch,
        ],
        compiler_params=pltpu.CompilerParams(vmem_limit_bytes=limit),
        name=kernel.__name__,
        cost_estimate=COST.get(kernel.__name__),
    )(*operands)


def flipped(block, mask, port=0):
    route = [(i, i ^ mask ^ (port if i & 1 else 0)) for i in range(lax.axis_size("node"))]
    return lax.ppermute(block, "node", route)


def fast_body(amplitudes, gates):
    total = amplitudes.shape[1]
    rows = total // LANES
    eighth, part16 = rows // 8, rows // 16
    me = lax.axis_index("node").astype(jnp.int32).reshape(1)
    x = amplitudes.reshape(2, rows, LANES).transpose(1, 0, 2).reshape(2 * rows, LANES)
    interleaved = (pltpu.VMEM((2 * rows, LANES), F32), pltpu.SemaphoreType.DMA((2,)))
    one, two = shape(2, eighth, LANES), shape(2, 2, eighth, LANES)
    q2, q1, own3, own0, give = call(
        first_kernel,
        (0, 1, 2, 3),
        [two, two, one, one, two],
        rows,
        [me, x, gates],
        [SMEM, HBM, HBM],
        interleaved,
        limit=532 * 104858,
    )
    recv = flipped(give, 1)
    r1, r2 = flipped(q1, 2), flipped(q2, 4)
    p0, p3 = call(before_lower, (4, 5, 8), [two, two], 4 * eighth, [own0, own3, recv, gates], [VMEM] * 4)
    r3 = flipped(p3, 6)
    weights = [jax.ShapeDtypeStruct((2, PAIR, PAIR), BF16)] * 2
    near, send1, send2, *w = call(after_lower, (4, 5, 8), [two, one, one, *weights], 4 * eighth, [r1, r2, gates], [VMEM] * 3)
    post1, post2 = flipped(send1, 1), flipped(send2, 1)
    block = (2, part16, LANES)
    own, give, y1, self0 = call(
        second_kernel,
        (6, 7),
        [shape(3, 2, *block), shape(8, *block), shape(*block), shape(*block)],
        rows,
        [me, p0, near, r3, post1, post2, *w],
        [SMEM] + [VMEM] * 7,
    )
    recv = flipped(give, 1)
    ready = call(
        before_kernel, (9,), [shape(2, *block)] * 2, 4 * part16, [own[2], recv[4:6], gates], [VMEM] * 3
    )
    payloads = [jnp.stack([own[i], recv[2 * i : 2 * i + 2]], 1) for i in range(2)]
    a0, a1 = [flipped(payload, 2 * base, 2) for base, payload in zip(PORTS, payloads)]
    mine, late = [flipped(payload, 2 * PORTS[2] + f, 2) for f, payload in enumerate(ready)]
    y1 = flipped(jnp.stack([y1, recv[6]]), 2)
    keep, send, *w = call(
        after_kernel,
        (9,),
        [shape(8, *block), shape(4, *block), *weights],
        12 * part16,
        [a0, a1, y1, self0, recv[7], gates],
        [VMEM] * 6,
    )
    early = flipped(send, 1)
    far = call(join_kernel, (9,), [shape(4, *block)], 8, [mine, late], [VMEM] * 2)[0]
    out = call(
        third_kernel,
        (10, 11),
        [shape(2 * rows, LANES)],
        rows,
        [me, keep, early, far, *w],
        [SMEM] + [VMEM] * 5,
        (interleaved[0], pltpu.SemaphoreType.DMA((4,))),
        [HBM],
    )[0]
    return out.reshape(rows, 2, LANES).transpose(1, 0, 2).reshape(2, total)


def swapped(block, axis, apart):
    count = lax.axis_size(axis)
    route = []
    for low in range(count):
        high = low | 1 << apart
        if high != low and high < count:
            route += [(low, high), (high, low)]
    return lax.ppermute(block, axis, route)


def apply_gate(state, gate_pair, offset):
    total = state.shape[1]
    real_g, imag_g = (gate_pair[0], gate_pair[1])
    hp = lax.Precision.HIGHEST
    if offset == 0:
        view = state.reshape(2, total // 128, 128)
        real_in, imag_in = (view[0], view[1])
        real_out = jnp.einsum("ij,aj->ai", real_g, real_in, precision=hp) - jnp.einsum(
            "ij,aj->ai", imag_g, imag_in, precision=hp
        )
        imag_out = jnp.einsum("ij,aj->ai", real_g, imag_in, precision=hp) + jnp.einsum(
            "ij,aj->ai", imag_g, real_in, precision=hp
        )
        return jnp.stack([real_out, imag_out], 0).reshape(2, total)
    inner = 1 << offset
    outer = total // (128 * inner)
    folded = 1
    if inner < 128:
        folded = min(128 // inner, outer)
    view = state.reshape(2, outer // folded, folded, 128, inner)
    view = jnp.transpose(view, (0, 1, 3, 2, 4)).reshape(2, outer // folded, 128, folded * inner)
    real_in, imag_in = (view[0], view[1])
    real_out = jnp.einsum("ij,ajb->aib", real_g, real_in, precision=hp) - jnp.einsum(
        "ij,ajb->aib", imag_g, imag_in, precision=hp
    )
    imag_out = jnp.einsum("ij,ajb->aib", real_g, imag_in, precision=hp) + jnp.einsum(
        "ij,ajb->aib", imag_g, real_in, precision=hp
    )
    result = jnp.stack([real_out, imag_out], 0).reshape(2, outer // folded, 128, folded, inner)
    return jnp.transpose(result, (0, 1, 3, 2, 4)).reshape(2, total)


def run_gates(state, gates, indices, offsets):
    distinct = gates.shape[1]
    for index, offset in zip(indices, offsets):
        state = apply_gate(state, gates[:, index % distinct], offset)
    return state


def leave_alone(half):
    return half


def split_halves(state, position, bit):
    total = state.shape[1]
    mine = lax.axis_index("node") // (1 << bit) % 2
    view = state.reshape(2, total >> position + 1, 2, 1 << position)
    keep = lax.dynamic_index_in_dim(view, mine, 2, keepdims=False)
    other = lax.dynamic_index_in_dim(view, 1 - mine, 2, keepdims=False)
    return (mine, keep, other)


def join_halves(mine, keep, arrived, total):
    lower = jnp.where(mine == 0, keep, arrived)
    upper = jnp.where(mine == 0, arrived, keep)
    return jnp.stack([lower, upper], 2).reshape(2, total)


def enter_bit(state, position, bit, prepare):
    total = state.shape[1]
    mine, keep, other = split_halves(state, position, bit)
    other = prepare(other.reshape(2, total // 2)).reshape(keep.shape)
    arrived = swapped(other, "node", bit)
    keep = prepare(keep.reshape(2, total // 2)).reshape(arrived.shape)
    return join_halves(mine, keep, arrived, total)


def general_body(amplitudes, gates):
    total = amplitudes.shape[1]
    locq = total.bit_length() - 1
    devices_node = lax.axis_size("node")
    offsets = [0, (locq - 7) // 2, locq - 7, locq - 9]
    state = run_gates(amplitudes, gates, [0, 1, 2, 3], offsets)

    def early_gates(half):
        return run_gates(half, gates, [4, 5], offsets[:2])

    state = enter_bit(state, locq - 1, 0, early_gates)
    for bit in range(1, 3):
        state = enter_bit(state, locq - 1 - bit, bit, leave_alone)
    state = run_gates(state, gates, [6, 7], offsets[2:])
    blocks = state.reshape(2, devices_node, total // devices_node)
    blocks = lax.all_to_all(blocks, "node", split_axis=1, concat_axis=1, tiled=True)
    state = blocks.reshape(2, total)
    return run_gates(state, gates, [8, 9, 10, 11], offsets)


def body(amplitudes, gates):
    if amplitudes.shape[1] == 65536 and lax.axis_size("node") == 16 and gates.shape[1] == 12:
        return fast_body(amplitudes, gates)
    return general_body(amplitudes, gates)


def solution(mesh):
    in_specs = (P(None, ("paths", "node")), P())
    out_specs = P(None, ("paths", "node"))
    return jax.shard_map(body, mesh=mesh, in_specs=in_specs, out_specs=out_specs, check_vma=False)
```
